768 devices in a mesh: row: 32 (over z_lo, x, core), col: 8 (over y), rep: 3 (over z_hi).
Axes of the slice: x: 4, y: 8, z: 12 (z_hi: 3, z_lo: 4; z = z_hi * 4 + z_lo), core: 2. Of those that a mesh axis runs over, the one named last changes fastest.
Arguments:
- x_tiles: float32 [192, 24, 128, 128], P('row'), may hold values from -6 to 6
- x_mask: int32 [192, 24], P('row'), may hold values 0 or 1
- p_mask: int32 [192, 24], P('row', 'col'), may hold values 0 or 1
- q_mask: int32 [192, 24], P('row', ('col', 'rep')), may hold values 0 or 1
Outputs:
- x_next: float32 [192, 24, 128, 128], P('row', ('col', 'rep'))
The draws below stay inside these ranges and needn't reach their ends.
All inputs are finite; a program needn't handle non-finite values. No bound on the sum of `x_mask` or of `p_mask` or of `q_mask` on one device may be relied on, other than what follows from the above.
Results may differ from the reference program's by a relative error of at most 0.0033.
Values may be sent and summed in bfloat16 or wider, within the bound.
A program may use at most 128 MiB of HBM per device.

```python
import math
import jax
import jax.numpy as jnp
from jax import lax

TILE_ORDER = 128
BAND_WIDTH = 24
TILE_ROWS = 192


def place_ends(drawn, stream_key, smallest, largest):
    spot = [jax.random.randint(jax.random.fold_in(stream_key, axis), (), 0, length) for axis, length in enumerate(drawn.shape)]
    widest = drawn.shape.index(max(drawn.shape))
    neighbour = spot[:widest] + [(spot[widest] + 1) % drawn.shape[widest]] + spot[widest + 1:]
    return drawn.at[tuple(spot)].set(smallest).at[tuple(neighbour)].set(largest)


def level_of(key, dims, split, smallest, high):
    factor_of = 1.0
    for dim, shards_of in split:
        heights = jax.random.uniform(jax.random.fold_in(jax.random.fold_in(key, 6), dim), (shards_of,), jnp.float32, smallest / len(split), high / len(split))
        factor_of = factor_of * jnp.repeat(jnp.exp(heights), dims[dim] // shards_of).reshape((-1,) + (1,) * (len(dims) - 1 - dim))
    return factor_of


def noise(stream_key, shape, deviation, limit, split=(), held_as=jnp.bfloat16):
    array = deviation * jax.random.normal(stream_key, shape, jnp.float32)
    if split:
        array = array * level_of(stream_key, shape, split, -0.22, 0.18)
    return jnp.clip(array, -limit, limit).astype(held_as)


def setup_inputs(seed: int = 0) -> dict:
    key_list = jax.random.split(jax.random.key(seed), 5)
    return {
        "x_tiles": noise(key_list[0], (TILE_ROWS, BAND_WIDTH, TILE_ORDER, TILE_ORDER), 1.0, 6.0, ((0, 32),), jnp.float32),
        "x_mask": place_ends((jax.random.randint(key_list[1], (TILE_ROWS, BAND_WIDTH), 0, 3) < 2).astype(jnp.int32), jax.random.fold_in(key_list[1], 1), 0, 1),
        "p_mask": place_ends((jax.random.randint(key_list[2], (TILE_ROWS, BAND_WIDTH), 0, 3) < 2).astype(jnp.int32), jax.random.fold_in(key_list[2], 1), 0, 1),
        "q_mask": place_ends((jax.random.randint(key_list[3], (TILE_ROWS, BAND_WIDTH), 0, 3) < 2).astype(jnp.int32), jax.random.fold_in(key_list[3], 1), 0, 1),
    }


def band_product(left_band, right_band):
    band_width = left_band.shape[1]
    half_band = band_width // 2
    padded = jnp.pad(right_band, ((0, 0), (band_width, band_width), (0, 0), (0, 0)))
    accumulated = jnp.zeros(left_band.shape, left_band.dtype)
    for inner_pos in range(band_width):
        slice_start = band_width + half_band - inner_pos
        aligned = padded[:, slice_start:slice_start + band_width]
        rolled = jnp.roll(aligned, half_band - inner_pos, axis=0)
        accumulated = accumulated + jnp.einsum('nab,nwbc->nwac', left_band[:, inner_pos], rolled, precision=lax.Precision.HIGHEST)
    return accumulated

def to_bfloat(values):
    rounded = values.astype(jnp.bfloat16)
    return lax.optimization_barrier(rounded).astype(values.dtype)

def reference(x_tiles, x_mask, p_mask, q_mask):
    norm_factor = math.sqrt(TILE_ORDER * BAND_WIDTH)
    masked = x_tiles * x_mask.astype(x_tiles.dtype)[:, :, None, None]
    scaled = to_bfloat(masked / norm_factor)
    square = to_bfloat(band_product(scaled, scaled) * p_mask.astype(x_tiles.dtype)[:, :, None, None])
    keep_mask = q_mask.astype(x_tiles.dtype)[:, :, None, None]
    cube_sum = band_product(square, scaled) * keep_mask
    return keep_mask * (1.5 * masked - 0.5 * norm_factor * cube_sum)
```

```python
import math

import jax
import jax.numpy as jnp
from jax import lax
from jax.experimental import pallas as pl
from jax.experimental.pallas import tpu as pltpu
from jax.sharding import PartitionSpec as P

MESH = pl.DeviceIdType.MESH
F32, BF16 = jnp.float32, jnp.bfloat16


def kernel(T, BW, n_rows, xm, pm, qm, x_hbm, out, xf, S, R, L, Q, PM, C, fin,
           ld_sem, x_send, x_recv, sib_send, sib_recv, pm_send, pm_recv,
           r_send, r_recv, f_send, f_recv):
    row, c, p = lax.axis_index("row"), lax.axis_index("col"), lax.axis_index("rep")
    n_chip = n_rows // 2
    q, s = lax.div(row, 2), lax.rem(row, 2)
    norm = math.sqrt(T * BW)
    inv_norm = 1.0 / norm
    p_fwd = jnp.where(q == n_chip - 1, lax.rem(p + 1, 3), p)
    p_bwd = jnp.where(q == 0, lax.rem(p + 2, 3), p)
    fwd = (lax.rem(row + 2, n_rows), c, p_fwd)
    bwd = (lax.rem(row + n_rows - 2, n_rows), c, p_bwd)
    sib = (row + 1 - 2 * s, c, p)
    right = (row, lax.rem(c + 1, 8), p)
    left = (row, lax.rem(c + 7, 8), p)
    w_me = 3 * c + p

    for k in range(6):
        pltpu.make_async_copy(x_hbm.at[k], xf.at[k], ld_sem.at[k]).start()

    def band_of(src, a, e):
        return lax.rem(lax.rem(src + 2 * s, 8) + 8 - a, 8) + 8 * e

    barrier = pltpu.get_barrier_semaphore()
    for peer in (fwd, bwd, sib):
        pl.semaphore_signal(barrier, inc=1, device_id=peer, device_id_type=MESH)
    for d in range(1, 8):
        pl.semaphore_signal(barrier, inc=1, device_id=(row, lax.rem(c + d, 8), p), device_id_type=MESH)

    def source_of(i):
        return lax.rem(w_me + i % 2 + 8 - 2 * s, 8)

    for i in range(6):
        src = source_of(i)

        @pl.when(jnp.logical_not((src == c) & (i // 2 == p)))
        def _():
            pl.semaphore_signal(barrier, inc=1, device_id=(row, src, jnp.int32(i // 2)), device_id_type=MESH)

    targets = []
    n_out = jnp.int32(0)
    for a in range(2):
        for e in range(3):
            w = band_of(c, a, e)
            cd, pd = lax.div(w, 3), lax.rem(w, 3)
            own = (cd == c) & (pd == p)
            targets.append((cd, pd, own))
            n_out = n_out + jnp.where(own, 0, 1)

    PM[c] = jnp.zeros((8, T), F32)
    for wl in range(3):
        for a in range(2):
            PM[c, pl.ds(wl * 2 + a, 1), :] = jnp.full((1, T), pm[2 * p + a, wl].astype(F32), F32)
    R[3, pl.ds(0, 12 * T), :] = jnp.zeros((12 * T, T), BF16)
    R[0, pl.ds(24 * T, 12 * T), :] = jnp.zeros((12 * T, T), BF16)

    def tile(k, w):
        ok = (w >= 0) & (w < BW)
        wc = jnp.clip(w, 0, BW - 1)
        scale = jnp.where(ok, xm[k, wc].astype(F32) * inv_norm, 0.0)
        return (xf[k, wc] * scale).astype(BF16)

    for k in range(6):
        pltpu.make_async_copy(x_hbm.at[k], xf.at[k], ld_sem.at[k]).wait()

        @pl.loop(0, 6)
        def _(h):
            base = jnp.where(h < 3, 2 * p_fwd + 12 + 8 * h, 2 * p_bwd - 12 + 8 * (h - 2)) + c - 6 * s
            S[h, pl.ds(k * T, T), :] = tile(k, base - k)

    pl.semaphore_wait(barrier, 10 + n_out)

    def x_copy(h):
        m = h if h < 3 else h - 2
        place = (0 if h < 3 else 24) + 6 * s
        return pltpu.make_async_remote_copy(
            src_ref=S.at[h], dst_ref=R.at[m, pl.ds(pl.multiple_of(place * T, T), 6 * T)],
            send_sem=x_send.at[h], recv_sem=x_recv.at[h],
            device_id=fwd if h < 3 else bwd, device_id_type=MESH)

    for h in (0, 3, 1, 4, 2, 5):
        x_copy(h).start()

    def pm_copy(d):
        return pltpu.make_async_remote_copy(
            src_ref=PM.at[c], dst_ref=PM.at[c], send_sem=pm_send.at[d - 1], recv_sem=pm_recv.at[d - 1],
            device_id=(row, lax.rem(c + d, 8), p), device_id_type=MESH)

    for d in range(1, 8):
        pm_copy(d).start()

    @pl.loop(0, 4)
    def _(m):
        for k in range(6):
            at = pl.multiple_of((12 + 6 * s + k) * T, T)
            R[m, pl.ds(at, T), :] = tile(k, 2 * p + c - 6 * s + 8 * m - k)

    def sib_copy(i, half):
        if i < 4:
            m, place = i, 12
        else:
            h = i - 4
            m, place = (h, 0) if h < 3 else (h - 2, 24)
        part = R.at[m, pl.ds(pl.multiple_of((place + 6 * half) * T, T), 6 * T)]
        return pltpu.make_async_remote_copy(
            src_ref=part, dst_ref=part, send_sem=sib_send.at[i], recv_sem=sib_recv.at[i],
            device_id=sib, device_id_type=MESH)

    for m in range(4):
        sib_copy(m, s).start()

    @pl.loop(0, BW)
    def _(u):
        for a in range(2):
            L[a, :, pl.ds(pl.multiple_of(u * T, T), T)] = tile(2 * p + a, u)

    for d in range(1, 8):
        pm_copy(d).wait_recv()

    w0 = [band_of(c, a, 0) for a in range(2)]
    m0 = [lax.div(w0[a] + a + 6 * s - c, 8) for a in range(2)]

    def column(a, e):
        start = pl.multiple_of((6 * s + 2 * p + a) * T, T)
        return R[m0[a] + e, pl.ds(start, BW * T), :]

    def ring_copy(way, h, a, e, src):
        w = band_of(src, a, e)
        part = Q.at[a, :, pl.ds(pl.multiple_of(w * T, T), T)]
        j = a * 3 + e
        return pltpu.make_async_remote_copy(
            src_ref=part, dst_ref=part, send_sem=r_send.at[way, h - 1, j], recv_sem=r_recv.at[way, h - 1, j],
            device_id=right if way == 0 else left, device_id_type=MESH)

    def source(way, h):
        return lax.rem(c + 8 - (h - 1), 8) if way == 0 else lax.rem(c + h - 1, 8)

    def halves(way, h):
        return (0, 1) if h < 4 else (way,)

    def arrive(m):
        hs = ([m] if m < 3 else []) + ([m + 2] if m > 0 else [])
        for h in hs:
            x_copy(h).wait_recv()
            sib_copy(4 + h, s).start()
        return hs

    for e in range(3):
        ms = (0, 1) if e == 0 else (e + 1,)
        hss = [arrive(m) for m in ms]
        for m, hs in zip(ms, hss):
            sib_copy(m, 1 - s).wait_recv()
            for h in hs:
                sib_copy(4 + h, 1 - s).wait_recv()
        for a in range(2):
            acc = jnp.dot(L[a], column(a, e), preferred_element_type=F32)
            w = w0[a] + 8 * e
            keep = PM[lax.div(w, 3), pl.ds(lax.rem(w, 3) * 2 + a, 1), :]
            Q[a, :, pl.ds(pl.multiple_of(w * T, T), T)] = (acc * keep).astype(BF16)
            for way in range(2):
                ring_copy(way, 1, a, e, source(way, 1)).start()

    for h in range(1, 5):
        for e in range(3):
            for way in range(2):
                for a in halves(way, h):
                    ring_copy(way, h, a, e, source(way, h + 1)).wait_recv()
                    if h < 4 and a in halves(way, h + 1):
                        ring_copy(way, h + 1, a, e, source(way, h + 1)).start()

    for a in range(2):
        for e in range(3):
            j = a * 3 + e
            cd, pd, own = targets[j]
            value = jnp.dot(Q[a], column(a, e), preferred_element_type=F32).astype(BF16)
            C[j] = value

            @pl.when(own)
            def _():
                fin[2 * p + a] = value

            @pl.when(jnp.logical_not(own))
            def _():
                pltpu.make_async_remote_copy(
                    src_ref=C.at[j], dst_ref=fin.at[2 * p + a], send_sem=f_send.at[j],
                    recv_sem=f_recv.at[2 * p + a], device_id=(row, cd, pd), device_id_type=MESH).start()

    for i in range(6):
        @pl.when(jnp.logical_not((source_of(i) == c) & (i // 2 == p)))
        def _():
            pltpu.make_async_remote_copy(
                src_ref=C.at[0], dst_ref=fin.at[i], send_sem=f_send.at[0], recv_sem=f_recv.at[i],
                device_id=right, device_id_type=MESH).wait_recv()

        keep = qm[i, 0].astype(F32)
        masked = xf[i, w_me] * xm[i, w_me].astype(F32)
        out[i, 0] = keep * (1.5 * masked - (0.5 * norm) * fin[i].astype(F32))

    for h in range(6):
        x_copy(h).wait_send()
    for d in range(1, 8):
        pm_copy(d).wait_send()
    for i in range(10):
        sib_copy(i, s).wait_send()
    for h in range(1, 5):
        for e in range(3):
            for way in range(2):
                for a in halves(way, h):
                    ring_copy(way, h, a, e, source(way, h)).wait_send()
    for j in range(6):
        @pl.when(jnp.logical_not(targets[j][2]))
        def _():
            pltpu.make_async_remote_copy(
                src_ref=C.at[j], dst_ref=fin.at[0], send_sem=f_send.at[j], recv_sem=f_recv.at[0],
                device_id=right, device_id_type=MESH).wait_send()


def body(x_tiles, x_mask, p_mask, q_mask):
    rows, BW, T = x_tiles.shape[0], x_tiles.shape[1], x_tiles.shape[2]
    n_rows = lax.axis_size("row")
    dma = pltpu.SemaphoreType.DMA

    def run(*refs):
        kernel(T, BW, n_rows, *refs)

    return pl.pallas_call(
        run,
        out_shape=jax.ShapeDtypeStruct((rows, 1, T, T), F32),
        in_specs=[pl.BlockSpec(memory_space=pltpu.SMEM)] * 3 + [pl.BlockSpec(memory_space=pl.ANY)],
        out_specs=pl.BlockSpec(memory_space=pltpu.VMEM),
        scratch_shapes=[
            pltpu.VMEM((rows, BW, T, T), F32),
            pltpu.VMEM((6, 6 * T, T), BF16),
            pltpu.VMEM((4, 36 * T, T), BF16),
            pltpu.VMEM((2, T, BW * T), BF16),
            pltpu.VMEM((2, T, BW * T), BF16),
            pltpu.VMEM((8, 8, T), F32),
            pltpu.VMEM((6, T, T), BF16),
            pltpu.VMEM((6, T, T), BF16),
            dma((6,)), dma((6,)), dma((6,)), dma((10,)), dma((10,)), dma((7,)), dma((7,)),
            dma((2, 4, 6)), dma((2, 4, 6)), dma((6,)), dma((6,)),
        ],
        compiler_params=pltpu.CompilerParams(
            collective_id=0, has_side_effects=True, vmem_limit_bytes=56 * 1024 * 1024),
        name="sign_step",
    )(x_mask, p_mask, q_mask, x_tiles)


def solution(mesh):
    in_specs = (
        P("row", None, None, None),
        P("row", None),
        P("row", "col"),
        P("row", ("col", "rep")),
    )
    out_specs = P("row", ("col", "rep"), None, None)
    return jax.shard_map(body, mesh=mesh, in_specs=in_specs, out_specs=out_specs, check_vma=False)
```

```python
import math

import jax
import jax.numpy as jnp
from jax import lax
from jax.experimental import pallas as pl
from jax.experimental.pallas import tpu as pltpu
from jax.sharding import PartitionSpec as P

MESH = pl.DeviceIdType.MESH
F32, BF16 = jnp.float32, jnp.bfloat16


def kernel(T, BW, n_rows, xm, pm, qm, x_hbm, out, xs, xo, xl, xf, S, R, L, Q, PM, C, fin,
           ls_sem, lo_sem, ll_sem, lf_sem, x_send, x_recv, sib_send, sib_recv, pm_send, pm_recv,
           r_send, r_recv, f_send, f_recv):
    row, c, p = lax.axis_index("row"), lax.axis_index("col"), lax.axis_index("rep")
    n_chip = n_rows // 2
    q, s = lax.div(row, 2), lax.rem(row, 2)
    norm = math.sqrt(T * BW)
    inv_norm = 1.0 / norm
    p_fwd = jnp.where(q == n_chip - 1, lax.rem(p + 1, 3), p)
    p_bwd = jnp.where(q == 0, lax.rem(p + 2, 3), p)
    fwd = (lax.rem(row + 2, n_rows), c, p_fwd)
    bwd = (lax.rem(row + n_rows - 2, n_rows), c, p_bwd)
    sib = (row + 1 - 2 * s, c, p)
    right = (row, lax.rem(c + 1, 8), p)
    left = (row, lax.rem(c + 7, 8), p)
    w_me = 3 * c + p

    def halo_base(h):
        return (2 * p_fwd + 12 + 8 * h if h < 3 else 2 * p_bwd - 12 + 8 * (h - 2)) + c - 6 * s

    def own_base(m):
        return 2 * p + c - 6 * s + 8 * m

    def load(base, buf, sem):
        @pl.loop(0, 6)
        def _(k):
            pltpu.make_async_copy(x_hbm.at[k, jnp.clip(base - k, 0, BW - 1)], buf.at[k], sem).start()

    def loaded(buf, sem):
        pltpu.make_async_copy(x_hbm.at[pl.ds(0, 6), 0], buf, sem).wait()

    for h in (1, 3):
        load(halo_base(h), xs.at[h], ls_sem.at[h])
    load(own_base(1), xo.at[1], lo_sem.at[1])
    for h in (2, 4):
        load(halo_base(h), xs.at[h], ls_sem.at[h])
    rows_copy = pltpu.make_async_copy(x_hbm.at[pl.ds(2 * p, 2)], xl, ll_sem)
    rows_copy.start()
    load(own_base(2), xo.at[2], lo_sem.at[2])
    for h in (0, 5):
        load(halo_base(h), xs.at[h], ls_sem.at[h])
    for m in (0, 3):
        load(own_base(m), xo.at[m], lo_sem.at[m])
    final_copy = pltpu.make_async_copy(x_hbm.at[pl.ds(0, 6), w_me], xf, lf_sem)
    final_copy.start()

    def first_of(src, a):
        return lax.rem(lax.rem(src + 2 * s, 8) + 8 - a, 8)

    barrier = pltpu.get_barrier_semaphore()
    for peer in (fwd, bwd, sib):
        pl.semaphore_signal(barrier, inc=1, device_id=peer, device_id_type=MESH)
    for d in range(1, 8):
        pl.semaphore_signal(barrier, inc=1, device_id=(row, lax.rem(c + d, 8), p), device_id_type=MESH)

    def source_of(i):
        return lax.rem(w_me + i % 2 + 8 - 2 * s, 8)

    for i in range(6):
        src = source_of(i)

        @pl.when(jnp.logical_not((src == c) & (i // 2 == p)))
        def _():
            pl.semaphore_signal(barrier, inc=1, device_id=(row, src, jnp.int32(i // 2)), device_id_type=MESH)

    targets = []
    n_out = jnp.int32(0)
    for a in range(2):
        for e in range(3):
            w = first_of(c, a) + 8 * e
            cd, pd = lax.div(w, 3), lax.rem(w, 3)
            own = (cd == c) & (pd == p)
            targets.append((cd, pd, own))
            n_out = n_out + jnp.where(own, 0, 1)

    def scale_of(k, w):
        ok = (w >= 0) & (w < BW)
        return jnp.where(ok, xm[k, jnp.clip(w, 0, BW - 1)].astype(F32) * inv_norm, 0.0)

    def make_halo(h):
        base = halo_base(h)
        loaded(xs.at[h], ls_sem.at[h])

        @pl.loop(0, 6)
        def _(k):
            S[h, pl.ds(pl.multiple_of(k * T, T), T), :] = (xs[h, k] * scale_of(k, base - k)).astype(BF16)

    def make_own(m):
        base = own_base(m)
        loaded(xo.at[m], lo_sem.at[m])

        @pl.loop(0, 6)
        def _(k):
            at = pl.multiple_of((12 + 6 * s + k) * T, T)
            R[m, pl.ds(at, T), :] = (xo[m, k] * scale_of(k, base - k)).astype(BF16)

    def x_copy(h):
        m = h if h < 3 else h - 2
        place = (0 if h < 3 else 24) + 6 * s
        return pltpu.make_async_remote_copy(
            src_ref=S.at[h], dst_ref=R.at[m, pl.ds(pl.multiple_of(place * T, T), 6 * T)],
            send_sem=x_send.at[h], recv_sem=x_recv.at[h],
            device_id=fwd if h < 3 else bwd, device_id_type=MESH)

    def pm_copy(d):
        return pltpu.make_async_remote_copy(
            src_ref=PM.at[c], dst_ref=PM.at[c], send_sem=pm_send.at[d - 1], recv_sem=pm_recv.at[d - 1],
            device_id=(row, lax.rem(c + d, 8), p), device_id_type=MESH)

    def sib_copy(i, half):
        if i < 4:
            m, place = i, 12
        else:
            h = i - 4
            m, place = (h, 0) if h < 3 else (h - 2, 24)
        part = R.at[m, pl.ds(pl.multiple_of((place + 6 * half) * T, T), 6 * T)]
        return pltpu.make_async_remote_copy(
            src_ref=part, dst_ref=part, send_sem=sib_send.at[i], recv_sem=sib_recv.at[i],
            device_id=sib, device_id_type=MESH)

    make_halo(1)
    make_halo(3)
    pl.semaphore_wait(barrier, 10 + n_out)
    x_copy(1).start()
    x_copy(3).start()
    PM[c] = jnp.zeros((8, T), F32)
    for wl in range(3):
        for a in range(2):
            PM[c, pl.ds(wl * 2 + a, 1), :] = jnp.full((1, T), pm[wl, 2 * p + a].astype(F32), F32)
    for d in range(1, 8):
        pm_copy(d).start()
    for h in (2, 4):
        make_halo(h)
        x_copy(h).start()
    make_own(1)
    sib_copy(1, s).start()
    for h in (0, 5):
        make_halo(h)
        x_copy(h).start()
    rows_copy.wait()

    @pl.loop(0, BW)
    def _(u):
        for a in range(2):
            L[a, :, pl.ds(pl.multiple_of(u * T, T), T)] = (xl[a, u] * scale_of(2 * p + a, u)).astype(BF16)

    for m in (2, 0, 3):
        make_own(m)
        sib_copy(m, s).start()
    R[3, pl.ds(0, 12 * T), :] = jnp.zeros((12 * T, T), BF16)
    R[0, pl.ds(24 * T, 12 * T), :] = jnp.zeros((12 * T, T), BF16)

    for d in range(1, 8):
        pm_copy(d).wait_recv()

    def place_of(src, a, o):
        w0 = first_of(src, a)
        m0 = lax.div(w0 + a + 6 * s - src, 8)
        e = (1 - m0, 2 - m0, 2 * m0)[o]
        return w0 + 8 * e, m0 + e

    def column(a, m):
        start = pl.multiple_of((6 * s + 2 * p + a) * T, T)
        return R[m, pl.ds(start, BW * T), :]

    def ring_copy(way, h, a, o, src):
        w, _ = place_of(src, a, o)
        part = Q.at[a, :, pl.ds(pl.multiple_of(w * T, T), T)]
        j = a * 3 + o
        return pltpu.make_async_remote_copy(
            src_ref=part, dst_ref=part, send_sem=r_send.at[way, h - 1, j], recv_sem=r_recv.at[way, h - 1, j],
            device_id=right if way == 0 else left, device_id_type=MESH)

    def source(way, h):
        return lax.rem(c + 8 - (h - 1), 8) if way == 0 else lax.rem(c + h - 1, 8)

    def halves(way, h):
        return (0, 1) if h < 4 else (way,)

    def square_round(o):
        hs, ms = (((1, 3), (1,)), ((2, 4), (2,)), ((0, 5), (0, 3)))[o]
        for h in hs:
            x_copy(h).wait_recv()
            sib_copy(4 + h, s).start()
        for m in ms:
            sib_copy(m, 1 - s).wait_recv()
        for h in hs:
            sib_copy(4 + h, 1 - s).wait_recv()
        for a in range(2):
            w, m = place_of(c, a, o)
            acc = jnp.dot(L[a], column(a, m), preferred_element_type=F32)
            keep = PM[lax.div(w, 3), pl.ds(lax.rem(w, 3) * 2 + a, 1), :]
            Q[a, :, pl.ds(pl.multiple_of(w * T, T), T)] = (acc * keep).astype(BF16)
            for way in range(2):
                ring_copy(way, 1, a, o, source(way, 1)).start()

    def ring_step(h, o):
        for way in range(2):
            for a in halves(way, h):
                ring_copy(way, h, a, o, source(way, h + 1)).wait_recv()
                if h < 4 and a in halves(way, h + 1):
                    ring_copy(way, h + 1, a, o, source(way, h + 1)).start()

    square_round(0)
    ring_step(1, 0)
    square_round(1)
    ring_step(2, 0)
    ring_step(1, 1)
    square_round(2)
    for h, o in ((3, 0), (2, 1), (1, 2), (4, 0), (3, 1), (2, 2), (4, 1), (3, 2), (4, 2)):
        ring_step(h, o)

    for a in range(2):
        for e in range(3):
            j = a * 3 + e
            cd, pd, own = targets[j]
            w0 = first_of(c, a)
            m = lax.div(w0 + a + 6 * s - c, 8) + e
            value = jnp.dot(Q[a], column(a, m), preferred_element_type=F32).astype(BF16)
            C[j] = value

            @pl.when(own)
            def _():
                fin[2 * p + a] = value

            @pl.when(jnp.logical_not(own))
            def _():
                pltpu.make_async_remote_copy(
                    src_ref=C.at[j], dst_ref=fin.at[2 * p + a], send_sem=f_send.at[j],
                    recv_sem=f_recv.at[2 * p + a], device_id=(row, cd, pd), device_id_type=MESH).start()

    final_copy.wait()
    for i in range(6):
        @pl.when(jnp.logical_not((source_of(i) == c) & (i // 2 == p)))
        def _():
            pltpu.make_async_remote_copy(
                src_ref=C.at[0], dst_ref=fin.at[i], send_sem=f_send.at[0], recv_sem=f_recv.at[i],
                device_id=right, device_id_type=MESH).wait_recv()

        keep = qm[0, i].astype(F32)
        masked = xf[i] * xm[i, w_me].astype(F32)
        out[i, 0] = keep * (1.5 * masked - (0.5 * norm) * fin[i].astype(F32))

    for h in range(6):
        x_copy(h).wait_send()
    for d in range(1, 8):
        pm_copy(d).wait_send()
    for i in range(10):
        sib_copy(i, s).wait_send()
    for h in range(1, 5):
        for o in range(3):
            for way in range(2):
                for a in halves(way, h):
                    ring_copy(way, h, a, o, source(way, h)).wait_send()
    for j in range(6):
        @pl.when(jnp.logical_not(targets[j][2]))
        def _():
            pltpu.make_async_remote_copy(
                src_ref=C.at[j], dst_ref=fin.at[0], send_sem=f_send.at[j], recv_sem=f_recv.at[0],
                device_id=right, device_id_type=MESH).wait_send()


def body(x_tiles, x_mask, p_mask, q_mask):
    rows, BW, T = x_tiles.shape[0], x_tiles.shape[1], x_tiles.shape[2]
    n_rows = lax.axis_size("row")
    dma = pltpu.SemaphoreType.DMA

    def run(*refs):
        kernel(T, BW, n_rows, *refs)

    return pl.pallas_call(
        run,
        out_shape=jax.ShapeDtypeStruct((rows, 1, T, T), F32),
        in_specs=[pl.BlockSpec(memory_space=pltpu.SMEM)] * 3 + [pl.BlockSpec(memory_space=pl.ANY)],
        out_specs=pl.BlockSpec(memory_space=pltpu.VMEM),
        scratch_shapes=[
            pltpu.VMEM((6, 6, T, T), F32),
            pltpu.VMEM((4, 6, T, T), F32),
            pltpu.VMEM((2, BW, T, T), F32),
            pltpu.VMEM((6, T, T), F32),
            pltpu.VMEM((6, 6 * T, T), BF16),
            pltpu.VMEM((4, 36 * T, T), BF16),
            pltpu.VMEM((2, T, BW * T), BF16),
            pltpu.VMEM((2, T, BW * T), BF16),
            pltpu.VMEM((8, 8, T), F32),
            pltpu.VMEM((6, T, T), BF16),
            pltpu.VMEM((6, T, T), BF16),
            dma((6,)), dma((4,)), dma, dma, dma((6,)), dma((6,)), dma((10,)), dma((10,)), dma((7,)), dma((7,)),
            dma((2, 4, 6)), dma((2, 4, 6)), dma((6,)), dma((6,)),
        ],
        compiler_params=pltpu.CompilerParams(
            collective_id=0, has_side_effects=True, vmem_limit_bytes=56 * 1024 * 1024),
        name="sign_step",
    )(x_mask, p_mask.T, q_mask.reshape(1, rows), x_tiles)


def solution(mesh):
    in_specs = (
        P("row", None, None, None),
        P("row", None),
        P("row", "col"),
        P("row", ("col", "rep")),
    )
    out_specs = P("row", ("col", "rep"), None, None)
    return jax.shard_map(body, mesh=mesh, in_specs=in_specs, out_specs=out_specs, check_vma=False)
```

```python
import math

import jax
import jax.numpy as jnp
from jax import lax
from jax.experimental import pallas as pl
from jax.experimental.pallas import tpu as pltpu
from jax.sharding import PartitionSpec as P

MESH = pl.DeviceIdType.MESH
F32, BF16 = jnp.float32, jnp.bfloat16


def kernel(T, BW, n_rows, xm, pm, qm, x_hbm, out, xs, xo, xl, xf, S, R, L, Q, PM, C, fin,
           ls_sem, lo_sem, ll_sem, lf_sem, x_send, x_recv, sib_send, sib_recv, pass_send, pass_recv, pm_send, pm_recv,
           r_send, r_recv, f_send, f_recv):
    row, c, p = lax.axis_index("row"), lax.axis_index("col"), lax.axis_index("rep")
    n_chip = n_rows // 2
    q, s = lax.div(row, 2), lax.rem(row, 2)
    norm = math.sqrt(T * BW)
    inv_norm = 1.0 / norm
    p_fwd = jnp.where(q == n_chip - 1, lax.rem(p + 1, 3), p)
    p_bwd = jnp.where(q == 0, lax.rem(p + 2, 3), p)
    fwd = (lax.rem(row + 2, n_rows), c, p_fwd)
    bwd = (lax.rem(row + n_rows - 2, n_rows), c, p_bwd)
    sib = (row + 1 - 2 * s, c, p)

    def beside(d):
        return (row, lax.rem(c + 8 + d, 8), p)

    w_me = 3 * c + p

    def base_of(h, rep, core):
        return (2 * rep + 12 + 8 * h if h < 3 else 2 * rep - 12 + 8 * (h - 2)) + c - 6 * core

    def needed(h, k, rep, core):
        w = base_of(h, rep, core) - k
        near = 6 * core + k >= 2 * rep if h < 3 else 6 * core + k <= 6 + 2 * rep
        return (w >= 0) & (w < BW) & near

    def halo_rep(h):
        return p_fwd if h < 3 else p_bwd

    def halo_base(h):
        return base_of(h, halo_rep(h), s)

    def own_base(m):
        return 2 * p + c - 6 * s + 8 * m

    def load(base, buf, sem):
        @pl.loop(0, 6)
        def _(k):
            pltpu.make_async_copy(x_hbm.at[k, jnp.clip(base - k, 0, BW - 1)], buf.at[k], sem).start()

    def loaded(buf, sem):
        pltpu.make_async_copy(x_hbm.at[pl.ds(0, 6), 0], buf, sem).wait()

    for h in (1, 3):
        load(halo_base(h), xs.at[h], ls_sem.at[h])
    load(own_base(1), xo.at[1], lo_sem.at[1])
    for h in (2, 4):
        load(halo_base(h), xs.at[h], ls_sem.at[h])
    rows_copy = pltpu.make_async_copy(x_hbm.at[pl.ds(2 * p, 2)], xl, ll_sem)
    rows_copy.start()
    load(own_base(2), xo.at[2], lo_sem.at[2])
    for h in (0, 5):
        load(halo_base(h), xs.at[h], ls_sem.at[h])
    for m in (0, 3):
        load(own_base(m), xo.at[m], lo_sem.at[m])
    final_copy = pltpu.make_async_copy(x_hbm.at[pl.ds(0, 6), w_me], xf, lf_sem)
    final_copy.start()

    def first_of(src, a):
        return lax.rem(lax.rem(src + 2 * s, 8) + 8 - a, 8)

    barrier = pltpu.get_barrier_semaphore()
    for peer in (fwd, bwd, sib):
        pl.semaphore_signal(barrier, inc=1, device_id=peer, device_id_type=MESH)
    for d in range(1, 8):
        pl.semaphore_signal(barrier, inc=1, device_id=(row, lax.rem(c + d, 8), p), device_id_type=MESH)

    def source_of(i):
        return lax.rem(w_me + i % 2 + 8 - 2 * s, 8)

    for i in range(6):
        src = source_of(i)

        @pl.when(jnp.logical_not((src == c) & (i // 2 == p)))
        def _():
            pl.semaphore_signal(barrier, inc=1, device_id=(row, src, jnp.int32(i // 2)), device_id_type=MESH)

    targets = []
    n_out = jnp.int32(0)
    for a in range(2):
        for e in range(3):
            w = first_of(c, a) + 8 * e
            cd, pd = lax.div(w, 3), lax.rem(w, 3)
            own = (cd == c) & (pd == p)
            targets.append((cd, pd, own))
            n_out = n_out + jnp.where(own, 0, 1)

    def scale_of(k, w):
        ok = (w >= 0) & (w < BW)
        return jnp.where(ok, xm[k, jnp.clip(w, 0, BW - 1)].astype(F32) * inv_norm, 0.0)

    def make_halo(h):
        base = halo_base(h)
        loaded(xs.at[h], ls_sem.at[h])

        @pl.loop(0, 6)
        def _(k):
            @pl.when(needed(h, k, halo_rep(h), s))
            def _():
                S[h, pl.ds(pl.multiple_of(k * T, T), T), :] = (xs[h, k] * scale_of(k, base - k)).astype(BF16)

    def make_own(m):
        base = own_base(m)
        loaded(xo.at[m], lo_sem.at[m])

        @pl.loop(0, 6)
        def _(k):
            at = pl.multiple_of((12 + 6 * s + k) * T, T)
            R[m, pl.ds(at, T), :] = (xo[m, k] * scale_of(k, base - k)).astype(BF16)

    def part_of(h, k, core):
        m, place = (h, 0) if h < 3 else (h - 2, 24)
        return R.at[m, pl.ds(pl.multiple_of((place + 6 * core + k) * T, T), T)]

    def x_copy(h, k):
        return pltpu.make_async_remote_copy(
            src_ref=S.at[h, pl.ds(pl.multiple_of(k * T, T), T)], dst_ref=part_of(h, k, s),
            send_sem=x_send.at[h, k], recv_sem=x_recv.at[h, k],
            device_id=fwd if h < 3 else bwd, device_id_type=MESH)

    def each(h, rep, core, do, other=None):
        @pl.loop(0, 6)
        def _(k):
            need = needed(h, k, rep, core)

            @pl.when(need)
            def _():
                do(k)

            if other is not None:
                @pl.when(jnp.logical_not(need))
                def _():
                    other(k)

    def x_start(h):
        each(h, halo_rep(h), s, lambda k: x_copy(h, k).start())

    def pm_copy(d):
        return pltpu.make_async_remote_copy(
            src_ref=PM.at[c], dst_ref=PM.at[c], send_sem=pm_send.at[d - 1], recv_sem=pm_recv.at[d - 1],
            device_id=(row, lax.rem(c + d, 8), p), device_id_type=MESH)

    def sib_copy(m, core):
        part = R.at[m, pl.ds(pl.multiple_of((12 + 6 * core) * T, T), 6 * T)]
        return pltpu.make_async_remote_copy(
            src_ref=part, dst_ref=part, send_sem=sib_send.at[m], recv_sem=sib_recv.at[m],
            device_id=sib, device_id_type=MESH)

    def pass_copy(h, k, core):
        part = part_of(h, k, core)
        return pltpu.make_async_remote_copy(
            src_ref=part, dst_ref=part, send_sem=pass_send.at[h, k], recv_sem=pass_recv.at[h, k],
            device_id=sib, device_id_type=MESH)

    make_halo(1)
    make_halo(3)
    pl.semaphore_wait(barrier, 10 + n_out)
    x_start(1)
    x_start(3)
    PM[c] = jnp.zeros((8, T), F32)
    for wl in range(3):
        for a in range(2):
            PM[c, pl.ds(wl * 2 + a, 1), :] = jnp.full((1, T), pm[wl, 2 * p + a].astype(F32), F32)
    for d in range(1, 8):
        pm_copy(d).start()
    for h in (2, 4):
        make_halo(h)
        x_start(h)
    make_own(1)
    sib_copy(1, s).start()
    for h in (0, 5):
        make_halo(h)
        x_start(h)
    rows_copy.wait()

    @pl.loop(0, BW)
    def _(u):
        for a in range(2):
            L[a, :, pl.ds(pl.multiple_of(u * T, T), T)] = (xl[a, u] * scale_of(2 * p + a, u)).astype(BF16)

    for m in (2, 0, 3):
        make_own(m)
        sib_copy(m, s).start()
    R[3, pl.ds(0, 12 * T), :] = jnp.zeros((12 * T, T), BF16)
    R[0, pl.ds(24 * T, 12 * T), :] = jnp.zeros((12 * T, T), BF16)
    for h in range(6):
        for core in range(2):
            def clear(k):
                part_of(h, k, core)[...] = jnp.zeros((T, T), BF16)

            each(h, p, core, lambda k: None, clear)

    for d in range(1, 8):
        pm_copy(d).wait_recv()

    def place_of(src, a, o):
        w0 = first_of(src, a)
        m0 = lax.div(w0 + a + 6 * s - src, 8)
        e = (1 - m0, 2 - m0, 2 * m0)[o]
        return w0 + 8 * e, m0 + e

    def column(a, m):
        start = pl.multiple_of((6 * s + 2 * p + a) * T, T)
        return R[m, pl.ds(start, BW * T), :]

    def ring_copy(way, h, a, o, src):
        w, _ = place_of(src, a, o)
        part = Q.at[a, :, pl.ds(pl.multiple_of(w * T, T), T)]
        j = a * 3 + o
        d = 1 if h in (1, 3) else 2
        return pltpu.make_async_remote_copy(
            src_ref=part, dst_ref=part, send_sem=r_send.at[way, h - 1, j], recv_sem=r_recv.at[way, h - 1, j],
            device_id=beside(d if way == 0 else -d), device_id_type=MESH)

    def origin(way, h):
        return lax.rem(c + 8 - h if way == 0 else c + h, 8)

    def halves(way, h):
        return (0, 1) if h < 4 else (way,)

    def square_round(o):
        hs, ms = (((1, 3), (1,)), ((2, 4), (2,)), ((0, 5), (0, 3)))[o]
        for h in hs:
            def forward(k):
                x_copy(h, k).wait_recv()
                pass_copy(h, k, s).start()

            each(h, p, s, forward)
        for m in ms:
            sib_copy(m, 1 - s).wait_recv()
        for h in hs:
            each(h, p, 1 - s, lambda k: pass_copy(h, k, 1 - s).wait_recv())
        for a in range(2):
            w, m = place_of(c, a, o)
            acc = jnp.dot(L[a], column(a, m), preferred_element_type=F32)
            keep = PM[lax.div(w, 3), pl.ds(lax.rem(w, 3) * 2 + a, 1), :]
            Q[a, :, pl.ds(pl.multiple_of(w * T, T), T)] = (acc * keep).astype(BF16)
            for h in (2, 1):
                for way in range(2):
                    ring_copy(way, h, a, o, c).start()

    def ring_forward(o):
        for a in range(2):
            for way in range(2):
                src = origin(way, 2)
                ring_copy(way, 2, a, o, src).wait_recv()
                if a == way:
                    ring_copy(way, 4, a, o, src).start()
                ring_copy(way, 3, a, o, src).start()

    square_round(0)
    square_round(1)
    ring_forward(0)
    square_round(2)
    ring_forward(1)
    ring_forward(2)
    for o in range(3):
        for h in (1, 3, 4):
            for way in range(2):
                for a in halves(way, h):
                    ring_copy(way, h, a, o, origin(way, h)).wait_recv()

    for a in range(2):
        for e in range(3):
            j = a * 3 + e
            cd, pd, own = targets[j]
            w0 = first_of(c, a)
            m = lax.div(w0 + a + 6 * s - c, 8) + e
            value = jnp.dot(Q[a], column(a, m), preferred_element_type=F32).astype(BF16)
            C[j] = value

            @pl.when(own)
            def _():
                fin[2 * p + a] = value

            @pl.when(jnp.logical_not(own))
            def _():
                pltpu.make_async_remote_copy(
                    src_ref=C.at[j], dst_ref=fin.at[2 * p + a], send_sem=f_send.at[j],
                    recv_sem=f_recv.at[2 * p + a], device_id=(row, cd, pd), device_id_type=MESH).start()

    final_copy.wait()
    for i in range(6):
        @pl.when(jnp.logical_not((source_of(i) == c) & (i // 2 == p)))
        def _():
            pltpu.make_async_remote_copy(
                src_ref=C.at[0], dst_ref=fin.at[i], send_sem=f_send.at[0], recv_sem=f_recv.at[i],
                device_id=beside(1), device_id_type=MESH).wait_recv()

        keep = qm[0, i].astype(F32)
        masked = xf[i] * xm[i, w_me].astype(F32)
        out[i, 0] = keep * (1.5 * masked - (0.5 * norm) * fin[i].astype(F32))

    for h in range(6):
        each(h, halo_rep(h), s, lambda k: x_copy(h, k).wait_send())
        each(h, p, s, lambda k: pass_copy(h, k, s).wait_send())
    for d in range(1, 8):
        pm_copy(d).wait_send()
    for m in range(4):
        sib_copy(m, s).wait_send()
    for h in range(1, 5):
        for o in range(3):
            for way in range(2):
                for a in halves(way, h):
                    ring_copy(way, h, a, o, c).wait_send()
    for j in range(6):
        @pl.when(jnp.logical_not(targets[j][2]))
        def _():
            pltpu.make_async_remote_copy(
                src_ref=C.at[j], dst_ref=fin.at[0], send_sem=f_send.at[j], recv_sem=f_recv.at[0],
                device_id=beside(1), device_id_type=MESH).wait_send()


def body(x_tiles, x_mask, p_mask, q_mask):
    rows, BW, T = x_tiles.shape[0], x_tiles.shape[1], x_tiles.shape[2]
    n_rows = lax.axis_size("row")
    dma = pltpu.SemaphoreType.DMA

    def run(*refs):
        kernel(T, BW, n_rows, *refs)

    return pl.pallas_call(
        run,
        out_shape=jax.ShapeDtypeStruct((rows, 1, T, T), F32),
        in_specs=[pl.BlockSpec(memory_space=pltpu.SMEM)] * 3 + [pl.BlockSpec(memory_space=pl.ANY)],
        out_specs=pl.BlockSpec(memory_space=pltpu.VMEM),
        scratch_shapes=[
            pltpu.VMEM((6, 6, T, T), F32),
            pltpu.VMEM((4, 6, T, T), F32),
            pltpu.VMEM((2, BW, T, T), F32),
            pltpu.VMEM((6, T, T), F32),
            pltpu.VMEM((6, 6 * T, T), BF16),
            pltpu.VMEM((4, 36 * T, T), BF16),
            pltpu.VMEM((2, T, BW * T), BF16),
            pltpu.VMEM((2, T, BW * T), BF16),
            pltpu.VMEM((8, 8, T), F32),
            pltpu.VMEM((6, T, T), BF16),
            pltpu.VMEM((6, T, T), BF16),
            dma((6,)), dma((4,)), dma, dma, dma((6, 6)), dma((6, 6)), dma((4,)), dma((4,)), dma((6, 6)), dma((6, 6)),
            dma((7,)), dma((7,)),
            dma((2, 4, 6)), dma((2, 4, 6)), dma((6,)), dma((6,)),
        ],
        compiler_params=pltpu.CompilerParams(
            collective_id=0, has_side_effects=True, vmem_limit_bytes=56 * 1024 * 1024),
        name="sign_step",
    )(x_mask, p_mask.T, q_mask.reshape(1, rows), x_tiles)


def solution(mesh):
    in_specs = (
        P("row", None, None, None),
        P("row", None),
        P("row", "col"),
        P("row", ("col", "rep")),
    )
    out_specs = P("row", ("col", "rep"), None, None)
    return jax.shard_map(body, mesh=mesh, in_specs=in_specs, out_specs=out_specs, check_vma=False)
```

```python
import math

import jax
import jax.numpy as jnp
from jax import lax
from jax.experimental import pallas as pl
from jax.experimental.pallas import tpu as pltpu
from jax.sharding import PartitionSpec as P

MESH = pl.DeviceIdType.MESH
F32, BF16 = jnp.float32, jnp.bfloat16


def kernel(T, BW, n_rows, xm, pm, qm, x_hbm, out, xs, xo, xl, xf, S, R, L, Q, PM, C, fin, ob,
           ls_sem, lo_sem, ll_sem, lf_sem, x_send, x_recv, sib_send, sib_recv, pass_send, pass_recv,
           pm_send, pm_recv, r_send, r_recv, f_send, f_recv, o_sem):
    row, c, p = lax.axis_index("row"), lax.axis_index("col"), lax.axis_index("rep")
    n_chip = n_rows // 2
    q, s = lax.div(row, 2), lax.rem(row, 2)
    norm = math.sqrt(T * BW)
    inv_norm = 1.0 / norm
    p_fwd = jnp.where(q == n_chip - 1, lax.rem(p + 1, 3), p)
    p_bwd = jnp.where(q == 0, lax.rem(p + 2, 3), p)

    def fwd(core):
        return (2 * lax.rem(q + 1, n_chip) + core, c, p_fwd)

    def bwd(core):
        return (2 * lax.rem(q + n_chip - 1, n_chip) + core, c, p_bwd)

    sib = (row + 1 - 2 * s, c, p)
    right = (row, lax.rem(c + 1, 8), p)
    left = (row, lax.rem(c + 7, 8), p)
    w_me = 3 * c + p

    def halo_rep(h):
        return p_fwd if h < 3 else p_bwd

    def needed(h, rep, core):
        v = c + 2 * rep
        return (None, v <= 8 + 6 * core, v <= 6 * core, v >= 4 + 6 * core, v >= 2 * core, c <= 6)[h]

    def on(h, rep, core, do):
        need = needed(h, rep, core)
        if need is None:
            do(0, 6)
        elif h in (2, 3):
            few = 0 if h == 2 else 1

            @pl.when(need & (core != few))
            def _():
                do(0, 6)

            @pl.when(need & (core == few))
            def _():
                do(*((5, 1) if h == 2 else (0, 2)))
        else:
            @pl.when(need)
            def _():
                do(0, 6)

    def halo_base(h):
        return (2 * p_fwd + 12 + 8 * h if h < 3 else 2 * p_bwd - 12 + 8 * (h - 2)) + c - 6 * s

    def own_base(m):
        return 2 * p + c - 6 * s + 8 * m

    def load(base, buf, sem):
        @pl.loop(0, 6)
        def _(k):
            pltpu.make_async_copy(x_hbm.at[k, jnp.clip(base - k, 0, BW - 1)], buf.at[k], sem).start()

    def loaded(buf, sem):
        pltpu.make_async_copy(x_hbm.at[pl.ds(0, 6), 0], buf, sem).wait()

    for h in (1, 3):
        load(halo_base(h), xs.at[h], ls_sem.at[h])
    load(own_base(1), xo.at[1], lo_sem.at[1])
    for h in (2, 4):
        load(halo_base(h), xs.at[h], ls_sem.at[h])
    rows_copy = pltpu.make_async_copy(x_hbm.at[pl.ds(2 * p, 2)], xl, ll_sem)
    rows_copy.start()
    load(own_base(2), xo.at[2], lo_sem.at[2])
    for h in (0, 5):
        load(halo_base(h), xs.at[h], ls_sem.at[h])
    for m in (0, 3):
        load(own_base(m), xo.at[m], lo_sem.at[m])
    final_copy = pltpu.make_async_copy(x_hbm.at[pl.ds(0, 6), w_me], xf, lf_sem)
    final_copy.start()

    def first_of(src, a):
        return lax.rem(lax.rem(src + 2 * s, 8) + 8 - a, 8)

    barrier = pltpu.get_barrier_semaphore()
    for peer in (fwd(0), fwd(1), bwd(0), bwd(1), sib):
        pl.semaphore_signal(barrier, inc=1, device_id=peer, device_id_type=MESH)
    for d in range(1, 8):
        pl.semaphore_signal(barrier, inc=1, device_id=(row, lax.rem(c + d, 8), p), device_id_type=MESH)

    def source_of(i):
        return lax.rem(w_me + i % 2 + 8 - 2 * s, 8)

    for i in range(6):
        src = source_of(i)

        @pl.when(jnp.logical_not((src == c) & (i // 2 == p)))
        def _():
            pl.semaphore_signal(barrier, inc=1, device_id=(row, src, jnp.int32(i // 2)), device_id_type=MESH)

    targets = []
    n_out = jnp.int32(0)
    m_first = [lax.div(first_of(c, a) + a + 6 * s - c, 8) for a in range(2)]
    for a in range(2):
        e_last = lax.rem(2 * (p + 24 - first_of(c, a)), 3)
        for i in range(3):
            e = lax.rem(e_last + 1 + i, 3)
            w = first_of(c, a) + 8 * e
            cd, pd = lax.div(w, 3), lax.rem(w, 3)
            own = (cd == c) & (pd == p)
            targets.append((e, cd, pd, own))
            n_out = n_out + jnp.where(own, 0, 1)

    def scale_of(k, w):
        ok = (w >= 0) & (w < BW)
        return jnp.where(ok, xm[k, jnp.clip(w, 0, BW - 1)].astype(F32) * inv_norm, 0.0)

    def make_halo(h):
        base = halo_base(h)
        loaded(xs.at[h], ls_sem.at[h])

        @pl.loop(0, 6)
        def _(k):
            S[h, pl.ds(pl.multiple_of(k * T, T), T), :] = (xs[h, k] * scale_of(k, base - k)).astype(BF16)

    def make_own(m):
        base = own_base(m)
        loaded(xo.at[m], lo_sem.at[m])

        @pl.loop(0, 6)
        def _(k):
            at = pl.multiple_of((12 + 6 * s + k) * T, T)
            R[m, pl.ds(at, T), :] = (xo[m, k] * scale_of(k, base - k)).astype(BF16)

    def part_of(h, core, k, n):
        m, place = (h, 0) if h < 3 else (h - 2, 24)
        return R.at[m, pl.ds(pl.multiple_of((place + 6 * core + k) * T, T), n * T)]

    def x_copy(h, core, k, n):
        to = 0 if h == 0 else 1 if h == 5 else s
        return pltpu.make_async_remote_copy(
            src_ref=S.at[h, pl.ds(k * T, n * T)], dst_ref=part_of(h, core, k, n),
            send_sem=x_send.at[h], recv_sem=x_recv.at[h, core],
            device_id=fwd(to) if h < 3 else bwd(to), device_id_type=MESH)

    def x_start(h):
        on(h, halo_rep(h), s, lambda k, n: x_copy(h, s, k, n).start())

    def pass_copy(h, core, k, n):
        part = part_of(h, core, k, n)
        return pltpu.make_async_remote_copy(
            src_ref=part, dst_ref=part, send_sem=pass_send.at[h, core], recv_sem=pass_recv.at[h, core],
            device_id=sib, device_id_type=MESH)

    def pm_copy(d):
        return pltpu.make_async_remote_copy(
            src_ref=PM.at[c], dst_ref=PM.at[c], send_sem=pm_send.at[d - 1], recv_sem=pm_recv.at[d - 1],
            device_id=(row, lax.rem(c + d, 8), p), device_id_type=MESH)

    def sib_copy(m, core):
        part = R.at[m, pl.ds(pl.multiple_of((12 + 6 * core) * T, T), 6 * T)]
        return pltpu.make_async_remote_copy(
            src_ref=part, dst_ref=part, send_sem=sib_send.at[m], recv_sem=sib_recv.at[m],
            device_id=sib, device_id_type=MESH)

    make_halo(1)
    make_halo(3)
    pl.semaphore_wait(barrier, 12 + n_out)
    x_start(1)
    x_start(3)
    PM[c] = jnp.zeros((8, T), F32)
    for wl in range(3):
        for a in range(2):
            PM[c, pl.ds(wl * 2 + a, 1), :] = jnp.full((1, T), pm[wl, 2 * p + a].astype(F32), F32)
    for d in range(1, 8):
        pm_copy(d).start()
    for h in (2, 4):
        make_halo(h)
        x_start(h)
    make_own(1)
    sib_copy(1, s).start()
    for h in (0, 5):
        make_halo(h)
        x_start(h)
    rows_copy.wait()

    @pl.loop(0, BW)
    def _(u):
        for a in range(2):
            L[a, :, pl.ds(pl.multiple_of(u * T, T), T)] = (xl[a, u] * scale_of(2 * p + a, u)).astype(BF16)

    for m in (2, 0, 3):
        make_own(m)
        sib_copy(m, s).start()
    R[3, pl.ds(0, 12 * T), :] = jnp.zeros((12 * T, T), BF16)
    R[0, pl.ds(24 * T, 12 * T), :] = jnp.zeros((12 * T, T), BF16)
    R[2, pl.ds(0, 5 * T), :] = jnp.zeros((5 * T, T), BF16)
    R[1, pl.ds(32 * T, 4 * T), :] = jnp.zeros((4 * T, T), BF16)
    for h in range(1, 5):
        for core in range(2):
            k, n = (5, 1) if (h, core) == (2, 0) else (0, 2) if (h, core) == (3, 1) else (0, 6)

            @pl.when(jnp.logical_not(needed(h, p, core)))
            def _():
                part_of(h, core, k, n)[...] = jnp.zeros((n * T, T), BF16)

    for d in range(1, 8):
        pm_copy(d).wait_recv()

    def place_of(src, a, o):
        w0 = first_of(src, a)
        m0 = lax.div(w0 + a + 6 * s - src, 8)
        e = (1 - m0, 2 - m0, 2 * m0)[o]
        return w0 + 8 * e, m0 + e

    def column(a, m):
        start = pl.multiple_of((6 * s + 2 * p + a) * T, T)
        return R[m, pl.ds(start, BW * T), :]

    def ring_copy(way, h, a, o, src):
        w, _ = place_of(src, a, o)
        part = Q.at[a, :, pl.ds(pl.multiple_of(w * T, T), T)]
        j = a * 3 + o
        return pltpu.make_async_remote_copy(
            src_ref=part, dst_ref=part, send_sem=r_send.at[way, h - 1, j], recv_sem=r_recv.at[way, h - 1, j],
            device_id=right if way == 0 else left, device_id_type=MESH)

    def source(way, h):
        return lax.rem(c + 8 - (h - 1), 8) if way == 0 else lax.rem(c + h - 1, 8)

    def halves(way, h):
        return (0, 1) if h < 4 else (way,)

    def halo_round(o):
        hs, m = (((1, 3), 1), ((2, 4), 2))[o]
        for h in hs:
            def forward(k, n):
                x_copy(h, s, k, n).wait_recv()
                pass_copy(h, s, k, n).start()

            on(h, p, s, forward)
        sib_copy(m, 1 - s).wait_recv()
        for h in hs:
            on(h, p, 1 - s, lambda k, n: pass_copy(h, 1 - s, k, n).wait_recv())

    both0, both3 = c >= 6, c == 0

    def last_round():
        for h, core, use, both in ((0, 0, None, both0), (5, 1, c <= 6, both3)):
            mine = s == core

            @pl.when(mine if use is None else mine & use)
            def _():
                for half in (1, 0):
                    x_copy(h, half, 0, 6).wait_recv()

                    @pl.when(both)
                    def _():
                        pass_copy(h, half, 0, 6).start()

        for m in (0, 3):
            sib_copy(m, 1 - s).wait_recv()
        for h, core, both in ((0, 0, both0), (5, 1, both3)):
            @pl.when((s != core) & both)
            def _():
                for half in (1, 0):
                    pass_copy(h, half, 0, 6).wait_recv()

    def square_round(o):
        if o < 2:
            halo_round(o)
        else:
            last_round()
        for a in range(2):
            w, m = place_of(c, a, o)
            acc = jnp.dot(L[a], column(a, m), preferred_element_type=F32)
            keep = PM[lax.div(w, 3), pl.ds(lax.rem(w, 3) * 2 + a, 1), :]
            Q[a, :, pl.ds(pl.multiple_of(w * T, T), T)] = (acc * keep).astype(BF16)
            for way in range(2):
                ring_copy(way, 1, a, o, source(way, 1)).start()

    def ring_step(h, o):
        for way in range(2):
            for a in halves(way, h):
                ring_copy(way, h, a, o, source(way, h + 1)).wait_recv()
                if h < 4 and a in halves(way, h + 1):
                    ring_copy(way, h + 1, a, o, source(way, h + 1)).start()

    square_round(0)
    ring_step(1, 0)
    square_round(1)
    ring_step(2, 0)
    square_round(2)
    for h, o in ((1, 1), (1, 2), (2, 1), (3, 0), (2, 2), (4, 0), (3, 1), (3, 2), (4, 1), (4, 2)):
        ring_step(h, o)

    for i in range(3):
        for a in range(2):
            j = 3 * a + i
            e, cd, pd, own = targets[j]
            value = jnp.dot(Q[a], column(a, m_first[a] + e), preferred_element_type=F32).astype(BF16)
            C[j] = value

            @pl.when(own)
            def _():
                fin[2 * p + a] = value

            @pl.when(jnp.logical_not(own))
            def _():
                pltpu.make_async_remote_copy(
                    src_ref=C.at[j], dst_ref=fin.at[2 * p + a], send_sem=f_send.at[j],
                    recv_sem=f_recv.at[2 * p + a], device_id=(row, cd, pd), device_id_type=MESH).start()

    def out_copy(i):
        return pltpu.make_async_copy(ob.at[i], out.at[i, 0], o_sem.at[i])

    final_copy.wait()
    for i in range(6):
        @pl.when(jnp.logical_not((source_of(i) == c) & (i // 2 == p)))
        def _():
            pltpu.make_async_remote_copy(
                src_ref=C.at[0], dst_ref=fin.at[i], send_sem=f_send.at[0], recv_sem=f_recv.at[i],
                device_id=right, device_id_type=MESH).wait_recv()

        keep = qm[0, i].astype(F32)
        masked = xf[i] * xm[i, w_me].astype(F32)
        ob[i] = keep * (1.5 * masked - (0.5 * norm) * fin[i].astype(F32))
        out_copy(i).start()

    for h in range(6):
        on(h, halo_rep(h), s, lambda k, n: x_copy(h, s, k, n).wait_send())
    for h in range(1, 5):
        on(h, p, s, lambda k, n: pass_copy(h, s, k, n).wait_send())
    for h, core, both in ((0, 0, both0), (5, 1, both3)):
        @pl.when((s == core) & both)
        def _():
            for half in range(2):
                pass_copy(h, half, 0, 6).wait_send()
    for d in range(1, 8):
        pm_copy(d).wait_send()
    for m in range(4):
        sib_copy(m, s).wait_send()
    for h in range(1, 5):
        for o in range(3):
            for way in range(2):
                for a in halves(way, h):
                    ring_copy(way, h, a, o, source(way, h)).wait_send()
    for j in range(6):
        @pl.when(jnp.logical_not(targets[j][3]))
        def _():
            pltpu.make_async_remote_copy(
                src_ref=C.at[j], dst_ref=fin.at[0], send_sem=f_send.at[j], recv_sem=f_recv.at[0],
                device_id=right, device_id_type=MESH).wait_send()
    for i in range(6):
        out_copy(i).wait()


def body(x_tiles, x_mask, p_mask, q_mask):
    rows, BW, T = x_tiles.shape[0], x_tiles.shape[1], x_tiles.shape[2]
    n_rows = lax.axis_size("row")
    dma = pltpu.SemaphoreType.DMA

    def run(*refs):
        kernel(T, BW, n_rows, *refs)

    return pl.pallas_call(
        run,
        out_shape=jax.ShapeDtypeStruct((rows, 1, T, T), F32),
        in_specs=[pl.BlockSpec(memory_space=pltpu.SMEM)] * 3 + [pl.BlockSpec(memory_space=pl.ANY)],
        out_specs=pl.BlockSpec(memory_space=pl.ANY),
        scratch_shapes=[
            pltpu.VMEM((6, 6, T, T), F32),
            pltpu.VMEM((4, 6, T, T), F32),
            pltpu.VMEM((2, BW, T, T), F32),
            pltpu.VMEM((6, T, T), F32),
            pltpu.VMEM((6, 6 * T, T), BF16),
            pltpu.VMEM((4, 36 * T, T), BF16),
            pltpu.VMEM((2, T, BW * T), BF16),
            pltpu.VMEM((2, T, BW * T), BF16),
            pltpu.VMEM((8, 8, T), F32),
            pltpu.VMEM((6, T, T), BF16),
            pltpu.VMEM((6, T, T), BF16),
            pltpu.VMEM((6, T, T), F32),
            dma((6,)), dma((4,)), dma, dma, dma((6,)), dma((6, 2)), dma((4,)), dma((4,)), dma((6, 2)), dma((6, 2)),
            dma((7,)), dma((7,)),
            dma((2, 4, 6)), dma((2, 4, 6)), dma((6,)), dma((6,)), dma((6,)),
        ],
        compiler_params=pltpu.CompilerParams(
            collective_id=0, has_side_effects=True, vmem_limit_bytes=56 * 1024 * 1024),
        name="sign_step",
    )(x_mask, p_mask.T, q_mask.reshape(1, rows), x_tiles)


def solution(mesh):
    in_specs = (
        P("row", None, None, None),
        P("row", None),
        P("row", "col"),
        P("row", ("col", "rep")),
    )
    out_specs = P("row", ("col", "rep"), None, None)
    return jax.shard_map(body, mesh=mesh, in_specs=in_specs, out_specs=out_specs, check_vma=False)
```

```python
import math

import jax
import jax.numpy as jnp
from jax import lax
from jax.experimental import pallas as pl
from jax.experimental.pallas import tpu as pltpu
from jax.sharding import PartitionSpec as P

MESH = pl.DeviceIdType.MESH
F32, BF16 = jnp.float32, jnp.bfloat16


def kernel(T, BW, n_rows, xm, pm, qm, x_hbm, out, xs, xo, xl, xf, S, R, L, Q, PM, C, fin, ob,
           ls_sem, lo_sem, ll_sem, lf_sem, x_send, x_recv, sib_send, sib_recv, pass_send, pass_recv,
           pm_send, pm_recv, r_send, r_recv, f_send, f_recv, o_sem):
    row, c, p = lax.axis_index("row"), lax.axis_index("col"), lax.axis_index("rep")
    n_chip = n_rows // 2
    q, s = lax.div(row, 2), lax.rem(row, 2)
    norm = math.sqrt(T * BW)
    inv_norm = 1.0 / norm
    p_fwd = jnp.where(q == n_chip - 1, lax.rem(p + 1, 3), p)
    p_bwd = jnp.where(q == 0, lax.rem(p + 2, 3), p)

    def fwd(core):
        return (2 * lax.rem(q + 1, n_chip) + core, c, p_fwd)

    def bwd(core):
        return (2 * lax.rem(q + n_chip - 1, n_chip) + core, c, p_bwd)

    sib = (row + 1 - 2 * s, c, p)
    right = (row, lax.rem(c + 1, 8), p)
    left = (row, lax.rem(c + 7, 8), p)
    w_me = 3 * c + p

    def halo_rep(h):
        return p_fwd if h < 3 else p_bwd

    def needed(h, rep, core):
        v = c + 2 * rep
        return (None, v <= 8 + 6 * core, v <= 6 * core, v >= 4 + 6 * core, v >= 2 * core, c <= 6)[h]

    def on(h, rep, core, do):
        need = needed(h, rep, core)
        if need is None:
            do(0, 6)
        elif h in (2, 3):
            few = 0 if h == 2 else 1

            @pl.when(need & (core != few))
            def _():
                do(0, 6)

            @pl.when(need & (core == few))
            def _():
                do(*((5, 1) if h == 2 else (0, 2)))
        else:
            @pl.when(need)
            def _():
                do(0, 6)

    def halo_base(h):
        return (2 * p_fwd + 12 + 8 * h if h < 3 else 2 * p_bwd - 12 + 8 * (h - 2)) + c - 6 * s

    def own_base(m):
        return 2 * p + c - 6 * s + 8 * m

    def load(base, buf, sem):
        @pl.loop(0, 6)
        def _(k):
            pltpu.make_async_copy(x_hbm.at[k, jnp.clip(base - k, 0, BW - 1)], buf.at[k], sem).start()

    def loaded(buf, sem):
        pltpu.make_async_copy(x_hbm.at[pl.ds(0, 6), 0], buf, sem).wait()

    for h in (1, 3):
        load(halo_base(h), xs.at[h], ls_sem.at[h])
    load(own_base(1), xo.at[1], lo_sem.at[1])
    for h in (2, 4):
        load(halo_base(h), xs.at[h], ls_sem.at[h])
    rows_copy = pltpu.make_async_copy(x_hbm.at[pl.ds(2 * p, 2)], xl, ll_sem)
    rows_copy.start()
    load(own_base(2), xo.at[2], lo_sem.at[2])
    for h in (0, 5):
        load(halo_base(h), xs.at[h], ls_sem.at[h])
    for m in (0, 3):
        load(own_base(m), xo.at[m], lo_sem.at[m])
    final_copy = pltpu.make_async_copy(x_hbm.at[pl.ds(0, 6), w_me], xf, lf_sem)
    final_copy.start()

    def first_of(src, a):
        return lax.rem(lax.rem(src + 2 * s, 8) + 8 - a, 8)

    barrier = pltpu.get_barrier_semaphore()
    for peer in (fwd(0), fwd(1), bwd(0), bwd(1), sib):
        pl.semaphore_signal(barrier, inc=1, device_id=peer, device_id_type=MESH)
    for d in range(1, 8):
        pl.semaphore_signal(barrier, inc=1, device_id=(row, lax.rem(c + d, 8), p), device_id_type=MESH)

    def source_of(i):
        return lax.rem(w_me + i % 2 + 8 - 2 * s, 8)

    for i in range(6):
        src = source_of(i)

        @pl.when(jnp.logical_not((src == c) & (i // 2 == p)))
        def _():
            pl.semaphore_signal(barrier, inc=1, device_id=(row, src, jnp.int32(i // 2)), device_id_type=MESH)

    targets = []
    n_out = jnp.int32(0)
    m_first = [lax.div(first_of(c, a) + a + 6 * s - c, 8) for a in range(2)]
    for a in range(2):
        e_last = lax.rem(2 * (p + 24 - first_of(c, a)), 3)
        for i in range(3):
            e = lax.rem(e_last + 1 + i, 3)
            w = first_of(c, a) + 8 * e
            cd, pd = lax.div(w, 3), lax.rem(w, 3)
            own = (cd == c) & (pd == p)
            targets.append((e, cd, pd, own))
            n_out = n_out + jnp.where(own, 0, 1)

    def scale_of(k, w):
        ok = (w >= 0) & (w < BW)
        return jnp.where(ok, xm[k, jnp.clip(w, 0, BW - 1)].astype(F32) * inv_norm, 0.0)

    def make_halo(h):
        base = halo_base(h)
        loaded(xs.at[h], ls_sem.at[h])

        @pl.loop(0, 6)
        def _(k):
            S[h, pl.ds(pl.multiple_of(k * T, T), T), :] = (xs[h, k] * scale_of(k, base - k)).astype(BF16)

    def make_own(m):
        base = own_base(m)
        loaded(xo.at[m], lo_sem.at[m])

        @pl.loop(0, 6)
        def _(k):
            at = pl.multiple_of((12 + 6 * s + k) * T, T)
            R[m, pl.ds(at, T), :] = (xo[m, k] * scale_of(k, base - k)).astype(BF16)

    def part_of(h, core, k, n):
        m, place = (h, 0) if h < 3 else (h - 2, 24)
        return R.at[m, pl.ds(pl.multiple_of((place + 6 * core + k) * T, T), n * T)]

    def x_copy(h, core, k, n):
        to = 0 if h == 0 else 1 if h == 5 else s
        return pltpu.make_async_remote_copy(
            src_ref=S.at[h, pl.ds(k * T, n * T)], dst_ref=part_of(h, core, k, n),
            send_sem=x_send.at[h], recv_sem=x_recv.at[h, core],
            device_id=fwd(to) if h < 3 else bwd(to), device_id_type=MESH)

    def x_start(h):
        on(h, halo_rep(h), s, lambda k, n: x_copy(h, s, k, n).start())

    def pass_copy(h, core, k, n):
        part = part_of(h, core, k, n)
        return pltpu.make_async_remote_copy(
            src_ref=part, dst_ref=part, send_sem=pass_send.at[h, core], recv_sem=pass_recv.at[h, core],
            device_id=sib, device_id_type=MESH)

    def pm_copy(d):
        return pltpu.make_async_remote_copy(
            src_ref=PM.at[c], dst_ref=PM.at[c], send_sem=pm_send.at[d - 1], recv_sem=pm_recv.at[d - 1],
            device_id=(row, lax.rem(c + d, 8), p), device_id_type=MESH)

    def sib_copy(m, core):
        part = R.at[m, pl.ds(pl.multiple_of((12 + 6 * core) * T, T), 6 * T)]
        return pltpu.make_async_remote_copy(
            src_ref=part, dst_ref=part, send_sem=sib_send.at[m], recv_sem=sib_recv.at[m],
            device_id=sib, device_id_type=MESH)

    make_halo(1)
    make_halo(3)
    pl.semaphore_wait(barrier, 12 + n_out)
    x_start(1)
    x_start(3)
    PM[c] = jnp.zeros((8, T), F32)
    for wl in range(3):
        for a in range(2):
            PM[c, pl.ds(wl * 2 + a, 1), :] = jnp.full((1, T), pm[wl, 2 * p + a].astype(F32), F32)
    for d in range(1, 8):
        pm_copy(d).start()
    for h in (2, 4):
        make_halo(h)
        x_start(h)
    make_own(1)
    sib_copy(1, s).start()
    for h in (0, 5):
        make_halo(h)
        x_start(h)
    rows_copy.wait()

    @pl.loop(0, BW)
    def _(u):
        for a in range(2):
            L[a, :, pl.ds(pl.multiple_of(u * T, T), T)] = (xl[a, u] * scale_of(2 * p + a, u)).astype(BF16)

    for m in (2, 0, 3):
        make_own(m)
        sib_copy(m, s).start()
    R[3, pl.ds(0, 12 * T), :] = jnp.zeros((12 * T, T), BF16)
    R[0, pl.ds(24 * T, 12 * T), :] = jnp.zeros((12 * T, T), BF16)
    R[2, pl.ds(0, 5 * T), :] = jnp.zeros((5 * T, T), BF16)
    R[1, pl.ds(32 * T, 4 * T), :] = jnp.zeros((4 * T, T), BF16)
    for h in range(1, 5):
        for core in range(2):
            k, n = (5, 1) if (h, core) == (2, 0) else (0, 2) if (h, core) == (3, 1) else (0, 6)

            @pl.when(jnp.logical_not(needed(h, p, core)))
            def _():
                part_of(h, core, k, n)[...] = jnp.zeros((n * T, T), BF16)

    for d in range(1, 8):
        pm_copy(d).wait_recv()

    def place_of(src, a, o):
        w0 = first_of(src, a)
        m0 = lax.div(w0 + a + 6 * s - src, 8)
        e = (1 - m0, 2 - m0, 2 * m0)[o]
        return w0 + 8 * e, m0 + e

    def column(a, m):
        start = pl.multiple_of((6 * s + 2 * p + a) * T, T)
        return R[m, pl.ds(start, BW * T), :]

    def ring_copy(way, h, a, o, src):
        w, _ = place_of(src, a, o)
        part = Q.at[a, :, pl.ds(pl.multiple_of(w * T, T), T)]
        j = a * 3 + o
        return pltpu.make_async_remote_copy(
            src_ref=part, dst_ref=part, send_sem=r_send.at[way, h - 1, j], recv_sem=r_recv.at[way, h - 1, j],
            device_id=right if way == 0 else left, device_id_type=MESH)

    def source(way, h):
        return lax.rem(c + 8 - (h - 1), 8) if way == 0 else lax.rem(c + h - 1, 8)

    def halves(way, h):
        return (0, 1) if h < 4 else (way,)

    def halo_round(o):
        hs, m = (((1, 3), 1), ((2, 4), 2))[o]
        for h in hs:
            def forward(k, n):
                x_copy(h, s, k, n).wait_recv()
                pass_copy(h, s, k, n).start()

            on(h, p, s, forward)
        sib_copy(m, 1 - s).wait_recv()
        for h in hs:
            on(h, p, 1 - s, lambda k, n: pass_copy(h, 1 - s, k, n).wait_recv())

    both0, both3 = c >= 6, c == 0

    def last_round():
        for h, core, use, both in ((0, 0, None, both0), (5, 1, c <= 6, both3)):
            mine = s == core

            @pl.when(mine if use is None else mine & use)
            def _():
                for half in (1, 0):
                    x_copy(h, half, 0, 6).wait_recv()

                    @pl.when(both)
                    def _():
                        pass_copy(h, half, 0, 6).start()

        for m in (0, 3):
            sib_copy(m, 1 - s).wait_recv()
        for h, core, both in ((0, 0, both0), (5, 1, both3)):
            @pl.when((s != core) & both)
            def _():
                for half in (1, 0):
                    pass_copy(h, half, 0, 6).wait_recv()

    def square_round(o):
        if o < 2:
            halo_round(o)
        else:
            last_round()
        for a in range(2):
            w, m = place_of(c, a, o)
            acc = jnp.dot(L[a], column(a, m), preferred_element_type=F32)
            keep = PM[lax.div(w, 3), pl.ds(lax.rem(w, 3) * 2 + a, 1), :]
            Q[a, :, pl.ds(pl.multiple_of(w * T, T), T)] = (acc * keep).astype(BF16)
            for way in range(2):
                ring_copy(way, 1, a, o, source(way, 1)).start()

    def ring_step(h, o):
        for way in range(2):
            for a in halves(way, h):
                ring_copy(way, h, a, o, source(way, h + 1)).wait_recv()
                if h < 4 and a in halves(way, h + 1):
                    ring_copy(way, h + 1, a, o, source(way, h + 1)).start()

    for o in range(3):
        square_round(o)
    for h in range(1, 5):
        for o in range(3):
            ring_step(h, o)

    for i in range(3):
        for a in range(2):
            j = 3 * a + i
            e, cd, pd, own = targets[j]
            value = jnp.dot(Q[a], column(a, m_first[a] + e), preferred_element_type=F32).astype(BF16)
            C[j] = value

            @pl.when(own)
            def _():
                fin[2 * p + a] = value

            @pl.when(jnp.logical_not(own))
            def _():
                pltpu.make_async_remote_copy(
                    src_ref=C.at[j], dst_ref=fin.at[2 * p + a], send_sem=f_send.at[j],
                    recv_sem=f_recv.at[2 * p + a], device_id=(row, cd, pd), device_id_type=MESH).start()

    def out_copy(i):
        return pltpu.make_async_copy(ob.at[i], out.at[i, 0], o_sem.at[i])

    final_copy.wait()
    for i in range(6):
        @pl.when(jnp.logical_not((source_of(i) == c) & (i // 2 == p)))
        def _():
            pltpu.make_async_remote_copy(
                src_ref=C.at[0], dst_ref=fin.at[i], send_sem=f_send.at[0], recv_sem=f_recv.at[i],
                device_id=right, device_id_type=MESH).wait_recv()

        keep = qm[0, i].astype(F32)
        masked = xf[i] * xm[i, w_me].astype(F32)
        ob[i] = keep * (1.5 * masked - (0.5 * norm) * fin[i].astype(F32))
        out_copy(i).start()

    for h in range(6):
        on(h, halo_rep(h), s, lambda k, n: x_copy(h, s, k, n).wait_send())
    for h in range(1, 5):
        on(h, p, s, lambda k, n: pass_copy(h, s, k, n).wait_send())
    for h, core, both in ((0, 0, both0), (5, 1, both3)):
        @pl.when((s == core) & both)
        def _():
            for half in range(2):
                pass_copy(h, half, 0, 6).wait_send()
    for d in range(1, 8):
        pm_copy(d).wait_send()
    for m in range(4):
        sib_copy(m, s).wait_send()
    for h in range(1, 5):
        for o in range(3):
            for way in range(2):
                for a in halves(way, h):
                    ring_copy(way, h, a, o, source(way, h)).wait_send()
    for j in range(6):
        @pl.when(jnp.logical_not(targets[j][3]))
        def _():
            pltpu.make_async_remote_copy(
                src_ref=C.at[j], dst_ref=fin.at[0], send_sem=f_send.at[j], recv_sem=f_recv.at[0],
                device_id=right, device_id_type=MESH).wait_send()
    for i in range(6):
        out_copy(i).wait()


def body(x_tiles, x_mask, p_mask, q_mask):
    rows, BW, T = x_tiles.shape[0], x_tiles.shape[1], x_tiles.shape[2]
    n_rows = lax.axis_size("row")
    dma = pltpu.SemaphoreType.DMA

    def run(*refs):
        kernel(T, BW, n_rows, *refs)

    return pl.pallas_call(
        run,
        out_shape=jax.ShapeDtypeStruct((rows, 1, T, T), F32),
        in_specs=[pl.BlockSpec(memory_space=pltpu.SMEM)] * 3 + [pl.BlockSpec(memory_space=pl.ANY)],
        out_specs=pl.BlockSpec(memory_space=pl.ANY),
        scratch_shapes=[
            pltpu.VMEM((6, 6, T, T), F32),
            pltpu.VMEM((4, 6, T, T), F32),
            pltpu.VMEM((2, BW, T, T), F32),
            pltpu.VMEM((6, T, T), F32),
            pltpu.VMEM((6, 6 * T, T), BF16),
            pltpu.VMEM((4, 36 * T, T), BF16),
            pltpu.VMEM((2, T, BW * T), BF16),
            pltpu.VMEM((2, T, BW * T), BF16),
            pltpu.VMEM((8, 8, T), F32),
            pltpu.VMEM((6, T, T), BF16),
            pltpu.VMEM((6, T, T), BF16),
            pltpu.VMEM((6, T, T), F32),
            dma((6,)), dma((4,)), dma, dma, dma((6,)), dma((6, 2)), dma((4,)), dma((4,)), dma((6, 2)), dma((6, 2)),
            dma((7,)), dma((7,)),
            dma((2, 4, 6)), dma((2, 4, 6)), dma((6,)), dma((6,)), dma((6,)),
        ],
        compiler_params=pltpu.CompilerParams(
            collective_id=0, has_side_effects=True, vmem_limit_bytes=56 * 1024 * 1024),
        name="sign_step",
    )(x_mask, p_mask.T, q_mask.reshape(1, rows), x_tiles)


def solution(mesh):
    in_specs = (
        P("row", None, None, None),
        P("row", None),
        P("row", "col"),
        P("row", ("col", "rep")),
    )
    out_specs = P("row", ("col", "rep"), None, None)
    return jax.shard_map(body, mesh=mesh, in_specs=in_specs, out_specs=out_specs, check_vma=False)
```

```python
import math

import jax
import jax.numpy as jnp
from jax import lax
from jax.experimental import pallas as pl
from jax.experimental.pallas import tpu as pltpu
from jax.sharding import PartitionSpec as P

MESH = pl.DeviceIdType.MESH
F32, BF16 = jnp.float32, jnp.bfloat16


def kernel(T, BW, n_rows, xm, pm, qm, x_hbm, out, xs, xo, xl, xf, S, R, L, Q, PM, C, fin, ob,
           ls_sem, lo_sem, ll_sem, lf_sem, x_send, x_recv, sib_send, sib_recv, pass_send, pass_recv,
           pm_send, pm_recv, r_send, r_recv, f_send, f_recv, o_sem):
    row, c, p = lax.axis_index("row"), lax.axis_index("col"), lax.axis_index("rep")
    n_chip = n_rows // 2
    q, s = lax.div(row, 2), lax.rem(row, 2)
    norm = math.sqrt(T * BW)
    inv_norm = 1.0 / norm
    p_fwd = jnp.where(q == n_chip - 1, lax.rem(p + 1, 3), p)
    p_bwd = jnp.where(q == 0, lax.rem(p + 2, 3), p)

    def fwd(core):
        return (2 * lax.rem(q + 1, n_chip) + core, c, p_fwd)

    def bwd(core):
        return (2 * lax.rem(q + n_chip - 1, n_chip) + core, c, p_bwd)

    sib = (row + 1 - 2 * s, c, p)
    right = (row, lax.rem(c + 1, 8), p)
    left = (row, lax.rem(c + 7, 8), p)
    w_me = 3 * c + p

    def halo_rep(h):
        return p_fwd if h < 3 else p_bwd

    def needed(h, rep, core):
        v = c + 2 * rep
        return (None, v <= 8 + 6 * core, v <= 6 * core, v >= 4 + 6 * core, v >= 2 * core, c <= 6)[h]

    def on(h, rep, core, do):
        need = needed(h, rep, core)
        if need is None:
            do(0, 6)
        elif h in (2, 3):
            few = 0 if h == 2 else 1

            @pl.when(need & (core != few))
            def _():
                do(0, 6)

            @pl.when(need & (core == few))
            def _():
                do(*((5, 1) if h == 2 else (0, 2)))
        else:
            @pl.when(need)
            def _():
                do(0, 6)

    def halo_base(h):
        return (2 * p_fwd + 12 + 8 * h if h < 3 else 2 * p_bwd - 12 + 8 * (h - 2)) + c - 6 * s

    def own_base(m):
        return 2 * p + c - 6 * s + 8 * m

    def load(base, buf, sem):
        @pl.loop(0, 6)
        def _(k):
            pltpu.make_async_copy(x_hbm.at[k, jnp.clip(base - k, 0, BW - 1)], buf.at[k], sem).start()

    def loaded(buf, sem):
        pltpu.make_async_copy(x_hbm.at[pl.ds(0, 6), 0], buf, sem).wait()

    def first_of(src, a):
        return lax.rem(lax.rem(src + 2 * s, 8) + 8 - a, 8)

    barrier = pltpu.get_barrier_semaphore()
    for peer in (fwd(0), fwd(1), bwd(0), bwd(1), sib):
        pl.semaphore_signal(barrier, inc=1, device_id=peer, device_id_type=MESH)
    for d in range(1, 8):
        pl.semaphore_signal(barrier, inc=1, device_id=(row, lax.rem(c + d, 8), p), device_id_type=MESH)

    def source_of(i):
        return lax.rem(w_me + i % 2 + 8 - 2 * s, 8)

    for i in range(6):
        src = source_of(i)

        @pl.when(jnp.logical_not((src == c) & (i // 2 == p)))
        def _():
            pl.semaphore_signal(barrier, inc=1, device_id=(row, src, jnp.int32(i // 2)), device_id_type=MESH)

    targets = []
    n_out = jnp.int32(0)
    m_first = [lax.div(first_of(c, a) + a + 6 * s - c, 8) for a in range(2)]
    for a in range(2):
        e_last = lax.rem(2 * (p + 24 - first_of(c, a)), 3)
        for i in range(3):
            e = lax.rem(e_last + 1 + i, 3)
            w = first_of(c, a) + 8 * e
            cd, pd = lax.div(w, 3), lax.rem(w, 3)
            own = (cd == c) & (pd == p)
            targets.append((e, cd, pd, own))
            n_out = n_out + jnp.where(own, 0, 1)

    for h in (1, 3, 2, 4):
        load(halo_base(h), xs.at[h], ls_sem.at[h])

    def scale_of(k, w):
        ok = (w >= 0) & (w < BW)
        return jnp.where(ok, xm[k, jnp.clip(w, 0, BW - 1)].astype(F32) * inv_norm, 0.0)

    def make_halo(h):
        base = halo_base(h)
        loaded(xs.at[h], ls_sem.at[h])

        @pl.loop(0, 6)
        def _(k):
            S[h, pl.ds(pl.multiple_of(k * T, T), T), :] = (xs[h, k] * scale_of(k, base - k)).astype(BF16)

    def make_own(m):
        base = own_base(m)
        loaded(xo.at[m], lo_sem.at[m])

        @pl.loop(0, 6)
        def _(k):
            at = pl.multiple_of((12 + 6 * s + k) * T, T)
            R[m, pl.ds(at, T), :] = (xo[m, k] * scale_of(k, base - k)).astype(BF16)

    def part_of(h, core, k, n):
        m, place = (h, 0) if h < 3 else (h - 2, 24)
        return R.at[m, pl.ds(pl.multiple_of((place + 6 * core + k) * T, T), n * T)]

    def x_copy(h, core, k, n):
        to = 0 if h == 0 else 1 if h == 5 else s
        return pltpu.make_async_remote_copy(
            src_ref=S.at[h, pl.ds(k * T, n * T)], dst_ref=part_of(h, core, k, n),
            send_sem=x_send.at[h], recv_sem=x_recv.at[h, core],
            device_id=fwd(to) if h < 3 else bwd(to), device_id_type=MESH)

    def x_start(h):
        on(h, halo_rep(h), s, lambda k, n: x_copy(h, s, k, n).start())

    def pass_copy(h, core, k, n):
        part = part_of(h, core, k, n)
        return pltpu.make_async_remote_copy(
            src_ref=part, dst_ref=part, send_sem=pass_send.at[h, core], recv_sem=pass_recv.at[h, core],
            device_id=sib, device_id_type=MESH)

    def pm_copy(d):
        return pltpu.make_async_remote_copy(
            src_ref=PM.at[c], dst_ref=PM.at[c], send_sem=pm_send.at[d - 1], recv_sem=pm_recv.at[d - 1],
            device_id=(row, lax.rem(c + d, 8), p), device_id_type=MESH)

    def sib_copy(m, core):
        part = R.at[m, pl.ds(pl.multiple_of((12 + 6 * core) * T, T), 6 * T)]
        return pltpu.make_async_remote_copy(
            src_ref=part, dst_ref=part, send_sem=sib_send.at[m], recv_sem=sib_recv.at[m],
            device_id=sib, device_id_type=MESH)

    make_halo(1)
    make_halo(3)
    pl.semaphore_wait(barrier, 12 + n_out)
    x_start(1)
    x_start(3)
    for h in (0, 5):
        load(halo_base(h), xs.at[h], ls_sem.at[h])
    load(own_base(1), xo.at[1], lo_sem.at[1])
    rows_copy = pltpu.make_async_copy(x_hbm.at[pl.ds(2 * p, 2)], xl, ll_sem)
    rows_copy.start()
    for m in (2, 0, 3):
        load(own_base(m), xo.at[m], lo_sem.at[m])
    final_copy = pltpu.make_async_copy(x_hbm.at[pl.ds(0, 6), w_me], xf, lf_sem)
    final_copy.start()
    PM[c] = jnp.zeros((8, T), F32)
    for wl in range(3):
        for a in range(2):
            PM[c, pl.ds(wl * 2 + a, 1), :] = jnp.full((1, T), pm[wl, 2 * p + a].astype(F32), F32)
    for d in range(1, 8):
        pm_copy(d).start()
    for h in (2, 4):
        make_halo(h)
        x_start(h)
    make_own(1)
    sib_copy(1, s).start()
    for h in (0, 5):
        make_halo(h)
        x_start(h)
    rows_copy.wait()

    @pl.loop(0, BW)
    def _(u):
        for a in range(2):
            L[a, :, pl.ds(pl.multiple_of(u * T, T), T)] = (xl[a, u] * scale_of(2 * p + a, u)).astype(BF16)

    for m in (2, 0, 3):
        make_own(m)
        sib_copy(m, s).start()
    R[3, pl.ds(0, 12 * T), :] = jnp.zeros((12 * T, T), BF16)
    R[0, pl.ds(24 * T, 12 * T), :] = jnp.zeros((12 * T, T), BF16)
    R[2, pl.ds(0, 5 * T), :] = jnp.zeros((5 * T, T), BF16)
    R[1, pl.ds(32 * T, 4 * T), :] = jnp.zeros((4 * T, T), BF16)
    for h in range(1, 5):
        for core in range(2):
            k, n = (5, 1) if (h, core) == (2, 0) else (0, 2) if (h, core) == (3, 1) else (0, 6)

            @pl.when(jnp.logical_not(needed(h, p, core)))
            def _():
                part_of(h, core, k, n)[...] = jnp.zeros((n * T, T), BF16)

    for d in range(1, 8):
        pm_copy(d).wait_recv()

    def place_of(src, a, o):
        w0 = first_of(src, a)
        m0 = lax.div(w0 + a + 6 * s - src, 8)
        e = (1 - m0, 2 - m0, 2 * m0)[o]
        return w0 + 8 * e, m0 + e

    def column(a, m):
        start = pl.multiple_of((6 * s + 2 * p + a) * T, T)
        return R[m, pl.ds(start, BW * T), :]

    def ring_copy(way, h, a, o, src):
        w, _ = place_of(src, a, o)
        part = Q.at[a, :, pl.ds(pl.multiple_of(w * T, T), T)]
        j = a * 3 + o
        return pltpu.make_async_remote_copy(
            src_ref=part, dst_ref=part, send_sem=r_send.at[way, h - 1, j], recv_sem=r_recv.at[way, h - 1, j],
            device_id=right if way == 0 else left, device_id_type=MESH)

    def source(way, h):
        return lax.rem(c + 8 - (h - 1), 8) if way == 0 else lax.rem(c + h - 1, 8)

    def halves(way, h):
        return (0, 1) if h < 4 else (way,)

    def halo_round(o):
        hs, m = (((1, 3), 1), ((2, 4), 2))[o]
        for h in hs:
            def forward(k, n):
                x_copy(h, s, k, n).wait_recv()
                pass_copy(h, s, k, n).start()

            on(h, p, s, forward)
        sib_copy(m, 1 - s).wait_recv()
        for h in hs:
            on(h, p, 1 - s, lambda k, n: pass_copy(h, 1 - s, k, n).wait_recv())

    both0, both3 = c >= 6, c == 0

    def last_round():
        for h, core, use, both in ((0, 0, None, both0), (5, 1, c <= 6, both3)):
            mine = s == core

            @pl.when(mine if use is None else mine & use)
            def _():
                for half in (1, 0):
                    x_copy(h, half, 0, 6).wait_recv()

                    @pl.when(both)
                    def _():
                        pass_copy(h, half, 0, 6).start()

        for m in (0, 3):
            sib_copy(m, 1 - s).wait_recv()
        for h, core, both in ((0, 0, both0), (5, 1, both3)):
            @pl.when((s != core) & both)
            def _():
                for half in (1, 0):
                    pass_copy(h, half, 0, 6).wait_recv()

    def square_round(o):
        if o < 2:
            halo_round(o)
        else:
            last_round()
        for a in range(2):
            w, m = place_of(c, a, o)
            acc = jnp.dot(L[a], column(a, m), preferred_element_type=F32)
            keep = PM[lax.div(w, 3), pl.ds(lax.rem(w, 3) * 2 + a, 1), :]
            Q[a, :, pl.ds(pl.multiple_of(w * T, T), T)] = (acc * keep).astype(BF16)
            for way in range(2):
                ring_copy(way, 1, a, o, source(way, 1)).start()

    def ring_step(h, a):
        for o in range(3):
            for way in range(2):
                if a in halves(way, h):
                    ring_copy(way, h, a, o, source(way, h + 1)).wait_recv()
                    if h < 4 and a in halves(way, h + 1):
                        ring_copy(way, h + 1, a, o, source(way, h + 1)).start()

    for o in range(3):
        square_round(o)
    def cube_row(a):
        for i in range(3):
            j = 3 * a + i
            e, cd, pd, own = targets[j]
            value = jnp.dot(Q[a], column(a, m_first[a] + e), preferred_element_type=F32).astype(BF16)
            C[j] = value

            @pl.when(own)
            def _():
                fin[2 * p + a] = value

            @pl.when(jnp.logical_not(own))
            def _():
                pltpu.make_async_remote_copy(
                    src_ref=C.at[j], dst_ref=fin.at[2 * p + a], send_sem=f_send.at[j],
                    recv_sem=f_recv.at[2 * p + a], device_id=(row, cd, pd), device_id_type=MESH).start()

    ring_step(1, 0)
    ring_step(1, 1)
    ring_step(2, 0)
    ring_step(2, 1)
    ring_step(3, 0)
    ring_step(3, 1)
    ring_step(4, 0)
    cube_row(0)
    ring_step(4, 1)
    cube_row(1)

    def out_copy(i):
        return pltpu.make_async_copy(ob.at[i], out.at[i, 0], o_sem.at[i])

    for h in range(6):
        on(h, halo_rep(h), s, lambda k, n: x_copy(h, s, k, n).wait_send())
    for h in range(1, 5):
        on(h, p, s, lambda k, n: pass_copy(h, s, k, n).wait_send())
    for h, core, both in ((0, 0, both0), (5, 1, both3)):
        @pl.when((s == core) & both)
        def _():
            for half in range(2):
                pass_copy(h, half, 0, 6).wait_send()
    for d in range(1, 8):
        pm_copy(d).wait_send()
    for m in range(4):
        sib_copy(m, s).wait_send()
    for h in range(1, 5):
        for o in range(3):
            for way in range(2):
                for a in halves(way, h):
                    ring_copy(way, h, a, o, source(way, h)).wait_send()
    final_copy.wait()
    for i in range(6):
        @pl.when(jnp.logical_not((source_of(i) == c) & (i // 2 == p)))
        def _():
            pltpu.make_async_remote_copy(
                src_ref=C.at[0], dst_ref=fin.at[i], send_sem=f_send.at[0], recv_sem=f_recv.at[i],
                device_id=right, device_id_type=MESH).wait_recv()

        keep = qm[0, i].astype(F32)
        masked = xf[i] * xm[i, w_me].astype(F32)
        ob[i] = keep * (1.5 * masked - (0.5 * norm) * fin[i].astype(F32))
        out_copy(i).start()

    for j in range(6):
        @pl.when(jnp.logical_not(targets[j][3]))
        def _():
            pltpu.make_async_remote_copy(
                src_ref=C.at[j], dst_ref=fin.at[0], send_sem=f_send.at[j], recv_sem=f_recv.at[0],
                device_id=right, device_id_type=MESH).wait_send()
    for i in range(6):
        out_copy(i).wait()


def body(x_tiles, x_mask, p_mask, q_mask):
    rows, BW, T = x_tiles.shape[0], x_tiles.shape[1], x_tiles.shape[2]
    n_rows = lax.axis_size("row")
    dma = pltpu.SemaphoreType.DMA

    def run(*refs):
        kernel(T, BW, n_rows, *refs)

    return pl.pallas_call(
        run,
        out_shape=jax.ShapeDtypeStruct((rows, 1, T, T), F32),
        in_specs=[pl.BlockSpec(memory_space=pltpu.SMEM)] * 3 + [pl.BlockSpec(memory_space=pl.ANY)],
        out_specs=pl.BlockSpec(memory_space=pl.ANY),
        scratch_shapes=[
            pltpu.VMEM((6, 6, T, T), F32),
            pltpu.VMEM((4, 6, T, T), F32),
            pltpu.VMEM((2, BW, T, T), F32),
            pltpu.VMEM((6, T, T), F32),
            pltpu.VMEM((6, 6 * T, T), BF16),
            pltpu.VMEM((4, 36 * T, T), BF16),
            pltpu.VMEM((2, T, BW * T), BF16),
            pltpu.VMEM((2, T, BW * T), BF16),
            pltpu.VMEM((8, 8, T), F32),
            pltpu.VMEM((6, T, T), BF16),
            pltpu.VMEM((6, T, T), BF16),
            pltpu.VMEM((6, T, T), F32),
            dma((6,)), dma((4,)), dma, dma, dma((6,)), dma((6, 2)), dma((4,)), dma((4,)), dma((6, 2)), dma((6, 2)),
            dma((7,)), dma((7,)),
            dma((2, 4, 6)), dma((2, 4, 6)), dma((6,)), dma((6,)), dma((6,)),
        ],
        compiler_params=pltpu.CompilerParams(
            collective_id=0, has_side_effects=True, vmem_limit_bytes=56 * 1024 * 1024),
        name="sign_step",
    )(x_mask, p_mask.T, q_mask.reshape(1, rows), x_tiles)


def solution(mesh):
    in_specs = (
        P("row", None, None, None),
        P("row", None),
        P("row", "col"),
        P("row", ("col", "rep")),
    )
    out_specs = P("row", ("col", "rep"), None, None)
    return jax.shard_map(body, mesh=mesh, in_specs=in_specs, out_specs=out_specs, check_vma=False)
```

```python
import math

import jax
import jax.numpy as jnp
from jax import lax
from jax.experimental import pallas as pl
from jax.experimental.pallas import tpu as pltpu
from jax.sharding import PartitionSpec as P

MESH = pl.DeviceIdType.MESH
F32, BF16 = jnp.float32, jnp.bfloat16


def kernel(T, BW, n_rows, xm, pm, qm, x_hbm, out, xs, xo, xl, xf, S, R, L, Q, PM, C, fin, ob,
           ls_sem, lo_sem, ll_sem, lf_sem, x_send, x_recv, sib_send, sib_recv, pass_send, pass_recv,
           pm_send, pm_recv, r_send, r_recv, f_send, f_recv, o_sem):
    row, c, p = lax.axis_index("row"), lax.axis_index("col"), lax.axis_index("rep")
    n_chip = n_rows // 2
    q, s = lax.div(row, 2), lax.rem(row, 2)
    norm = math.sqrt(T * BW)
    inv_norm = 1.0 / norm
    p_fwd = jnp.where(q == n_chip - 1, lax.rem(p + 1, 3), p)
    p_bwd = jnp.where(q == 0, lax.rem(p + 2, 3), p)

    def fwd(core):
        return (2 * lax.rem(q + 1, n_chip) + core, c, p_fwd)

    def bwd(core):
        return (2 * lax.rem(q + n_chip - 1, n_chip) + core, c, p_bwd)

    sib = (row + 1 - 2 * s, c, p)
    right = (row, lax.rem(c + 1, 8), p)
    left = (row, lax.rem(c + 7, 8), p)
    w_me = 3 * c + p

    def halo_rep(h):
        return p_fwd if h < 3 else p_bwd

    def needed(h, rep, core):
        v = c + 2 * rep
        return (None, v <= 8 + 6 * core, v <= 6 * core, v >= 4 + 6 * core, v >= 2 * core, c <= 6)[h]

    def on(h, rep, core, do):
        need = needed(h, rep, core)
        if need is None:
            do(0, 6)
        elif h in (2, 3):
            few = 0 if h == 2 else 1

            @pl.when(need & (core != few))
            def _():
                do(0, 6)

            @pl.when(need & (core == few))
            def _():
                do(*((5, 1) if h == 2 else (0, 2)))
        else:
            @pl.when(need)
            def _():
                do(0, 6)

    def halo_base(h):
        return (2 * p_fwd + 12 + 8 * h if h < 3 else 2 * p_bwd - 12 + 8 * (h - 2)) + c - 6 * s

    def own_base(m):
        return 2 * p + c - 6 * s + 8 * m

    def load(base, buf, sem):
        @pl.loop(0, 6)
        def _(k):
            pltpu.make_async_copy(x_hbm.at[k, jnp.clip(base - k, 0, BW - 1)], buf.at[k], sem).start()

    def loaded(buf, sem):
        pltpu.make_async_copy(x_hbm.at[pl.ds(0, 6), 0], buf, sem).wait()

    def first_of(src, a):
        return lax.rem(lax.rem(src + 2 * s, 8) + 8 - a, 8)

    barrier = pltpu.get_barrier_semaphore()
    for peer in (fwd(0), fwd(1), bwd(0), bwd(1), sib):
        pl.semaphore_signal(barrier, inc=1, device_id=peer, device_id_type=MESH)
    for d in range(1, 8):
        pl.semaphore_signal(barrier, inc=1, device_id=(row, lax.rem(c + d, 8), p), device_id_type=MESH)

    def source_of(i):
        return lax.rem(w_me + i % 2 + 8 - 2 * s, 8)

    for i in range(6):
        src = source_of(i)

        @pl.when(jnp.logical_not((src == c) & (i // 2 == p)))
        def _():
            pl.semaphore_signal(barrier, inc=1, device_id=(row, src, jnp.int32(i // 2)), device_id_type=MESH)

    targets = []
    n_out = jnp.int32(0)
    m_first = [lax.div(first_of(c, a) + a + 6 * s - c, 8) for a in range(2)]
    for a in range(2):
        e_last = lax.rem(2 * (p + 24 - first_of(c, a)), 3)
        for i in range(3):
            e = lax.rem(e_last + 1 + i, 3)
            w = first_of(c, a) + 8 * e
            cd, pd = lax.div(w, 3), lax.rem(w, 3)
            own = (cd == c) & (pd == p)
            targets.append((e, cd, pd, own))
            n_out = n_out + jnp.where(own, 0, 1)

    for h in (1, 3, 2, 4):
        load(halo_base(h), xs.at[h], ls_sem.at[h])

    def scale_of(k, w):
        ok = (w >= 0) & (w < BW)
        return jnp.where(ok, xm[k, jnp.clip(w, 0, BW - 1)].astype(F32) * inv_norm, 0.0)

    def make_halo(h):
        base = halo_base(h)
        loaded(xs.at[h], ls_sem.at[h])

        @pl.loop(0, 6)
        def _(k):
            S[h, pl.ds(pl.multiple_of(k * T, T), T), :] = (xs[h, k] * scale_of(k, base - k)).astype(BF16)

    def make_own(m):
        base = own_base(m)
        loaded(xo.at[m], lo_sem.at[m])

        @pl.loop(0, 6)
        def _(k):
            at = pl.multiple_of((12 + 6 * s + k) * T, T)
            R[m, pl.ds(at, T), :] = (xo[m, k] * scale_of(k, base - k)).astype(BF16)

    def part_of(h, core, k, n):
        m, place = (h, 0) if h < 3 else (h - 2, 24)
        return R.at[m, pl.ds(pl.multiple_of((place + 6 * core + k) * T, T), n * T)]

    def x_copy(h, core, k, n):
        to = 0 if h == 0 else 1 if h == 5 else s
        return pltpu.make_async_remote_copy(
            src_ref=S.at[h, pl.ds(k * T, n * T)], dst_ref=part_of(h, core, k, n),
            send_sem=x_send.at[h], recv_sem=x_recv.at[h, core],
            device_id=fwd(to) if h < 3 else bwd(to), device_id_type=MESH)

    def x_start(h):
        on(h, halo_rep(h), s, lambda k, n: x_copy(h, s, k, n).start())

    def pass_copy(h, core, k, n):
        part = part_of(h, core, k, n)
        return pltpu.make_async_remote_copy(
            src_ref=part, dst_ref=part, send_sem=pass_send.at[h, core], recv_sem=pass_recv.at[h, core],
            device_id=sib, device_id_type=MESH)

    def pm_copy(d):
        return pltpu.make_async_remote_copy(
            src_ref=PM.at[c], dst_ref=PM.at[c], send_sem=pm_send.at[d - 1], recv_sem=pm_recv.at[d - 1],
            device_id=(row, lax.rem(c + d, 8), p), device_id_type=MESH)

    def sib_copy(m, core):
        part = R.at[m, pl.ds(pl.multiple_of((12 + 6 * core) * T, T), 6 * T)]
        return pltpu.make_async_remote_copy(
            src_ref=part, dst_ref=part, send_sem=sib_send.at[m], recv_sem=sib_recv.at[m],
            device_id=sib, device_id_type=MESH)

    make_halo(1)
    make_halo(3)
    pl.semaphore_wait(barrier, 12 + n_out)
    x_start(1)
    x_start(3)
    for h in (0, 5):
        load(halo_base(h), xs.at[h], ls_sem.at[h])
    load(own_base(1), xo.at[1], lo_sem.at[1])
    rows_copy = pltpu.make_async_copy(x_hbm.at[pl.ds(2 * p, 2)], xl, ll_sem)
    rows_copy.start()
    for m in (2, 0, 3):
        load(own_base(m), xo.at[m], lo_sem.at[m])
    final_copy = pltpu.make_async_copy(x_hbm.at[pl.ds(0, 6), w_me], xf, lf_sem)
    final_copy.start()
    PM[c] = jnp.zeros((8, T), F32)
    for wl in range(3):
        for a in range(2):
            PM[c, pl.ds(wl * 2 + a, 1), :] = jnp.full((1, T), pm[wl, 2 * p + a].astype(F32), F32)
    for d in range(1, 8):
        pm_copy(d).start()
    for h in (2, 4):
        make_halo(h)
        x_start(h)
    make_own(1)
    sib_copy(1, s).start()
    for h in (0, 5):
        make_halo(h)
    rows_copy.wait()

    @pl.loop(0, BW)
    def _(u):
        for a in range(2):
            L[a, :, pl.ds(pl.multiple_of(u * T, T), T)] = (xl[a, u] * scale_of(2 * p + a, u)).astype(BF16)

    for h in (1, 3):
        on(h, halo_rep(h), s, lambda k, n: x_copy(h, s, k, n).wait_send())
    for h in (0, 5):
        x_start(h)
    for m in (2, 0, 3):
        make_own(m)
        sib_copy(m, s).start()
    R[3, pl.ds(0, 12 * T), :] = jnp.zeros((12 * T, T), BF16)
    R[0, pl.ds(24 * T, 12 * T), :] = jnp.zeros((12 * T, T), BF16)
    R[2, pl.ds(0, 5 * T), :] = jnp.zeros((5 * T, T), BF16)
    R[1, pl.ds(32 * T, 4 * T), :] = jnp.zeros((4 * T, T), BF16)
    for h in range(1, 5):
        for core in range(2):
            k, n = (5, 1) if (h, core) == (2, 0) else (0, 2) if (h, core) == (3, 1) else (0, 6)

            @pl.when(jnp.logical_not(needed(h, p, core)))
            def _():
                part_of(h, core, k, n)[...] = jnp.zeros((n * T, T), BF16)

    for d in range(1, 8):
        pm_copy(d).wait_recv()

    def place_of(src, a, o):
        w0 = first_of(src, a)
        m0 = lax.div(w0 + a + 6 * s - src, 8)
        e = (1 - m0, 2 - m0, 2 * m0)[o]
        return w0 + 8 * e, m0 + e

    def column(a, m):
        start = pl.multiple_of((6 * s + 2 * p + a) * T, T)
        return R[m, pl.ds(start, BW * T), :]

    def ring_copy(way, h, a, o, src):
        w, _ = place_of(src, a, o)
        part = Q.at[a, :, pl.ds(pl.multiple_of(w * T, T), T)]
        j = a * 3 + o
        return pltpu.make_async_remote_copy(
            src_ref=part, dst_ref=part, send_sem=r_send.at[way, h - 1, j], recv_sem=r_recv.at[way, h - 1, j],
            device_id=right if way == 0 else left, device_id_type=MESH)

    def source(way, h):
        return lax.rem(c + 8 - (h - 1), 8) if way == 0 else lax.rem(c + h - 1, 8)

    def halves(way, h):
        return (0, 1) if h < 4 else (way,)

    def halo_round(o):
        hs, m = (((1, 3), 1), ((2, 4), 2))[o]
        for h in hs:
            def forward(k, n):
                x_copy(h, s, k, n).wait_recv()
                pass_copy(h, s, k, n).start()

            on(h, p, s, forward)
        sib_copy(m, 1 - s).wait_recv()
        for h in hs:
            on(h, p, 1 - s, lambda k, n: pass_copy(h, 1 - s, k, n).wait_recv())

    both0, both3 = c >= 6, c == 0

    def last_round():
        for h, core, use, both in ((0, 0, None, both0), (5, 1, c <= 6, both3)):
            mine = s == core

            @pl.when(mine if use is None else mine & use)
            def _():
                for half in (1, 0):
                    x_copy(h, half, 0, 6).wait_recv()

                    @pl.when(both)
                    def _():
                        pass_copy(h, half, 0, 6).start()

        for m in (0, 3):
            sib_copy(m, 1 - s).wait_recv()
        for h, core, both in ((0, 0, both0), (5, 1, both3)):
            @pl.when((s != core) & both)
            def _():
                for half in (1, 0):
                    pass_copy(h, half, 0, 6).wait_recv()

    def square_round(o):
        if o < 2:
            halo_round(o)
        else:
            last_round()
        for a in range(2):
            w, m = place_of(c, a, o)
            acc = jnp.dot(L[a], column(a, m), preferred_element_type=F32)
            keep = PM[lax.div(w, 3), pl.ds(lax.rem(w, 3) * 2 + a, 1), :]
            Q[a, :, pl.ds(pl.multiple_of(w * T, T), T)] = (acc * keep).astype(BF16)
            for way in range(2):
                ring_copy(way, 1, a, o, source(way, 1)).start()

    def ring_step(h, a):
        for o in range(3):
            for way in range(2):
                if a in halves(way, h):
                    ring_copy(way, h, a, o, source(way, h + 1)).wait_recv()
                    if h < 4 and a in halves(way, h + 1):
                        ring_copy(way, h + 1, a, o, source(way, h + 1)).start()

    for o in range(3):
        square_round(o)
    def cube_row(a):
        for i in range(3):
            j = 3 * a + i
            e, cd, pd, own = targets[j]
            value = jnp.dot(Q[a], column(a, m_first[a] + e), preferred_element_type=F32).astype(BF16)
            C[j] = value

            @pl.when(own)
            def _():
                fin[2 * p + a] = value

            @pl.when(jnp.logical_not(own))
            def _():
                pltpu.make_async_remote_copy(
                    src_ref=C.at[j], dst_ref=fin.at[2 * p + a], send_sem=f_send.at[j],
                    recv_sem=f_recv.at[2 * p + a], device_id=(row, cd, pd), device_id_type=MESH).start()

    ring_step(1, 0)
    ring_step(1, 1)
    ring_step(2, 0)
    ring_step(2, 1)
    ring_step(3, 0)
    ring_step(3, 1)
    ring_step(4, 0)
    cube_row(0)
    ring_step(4, 1)
    cube_row(1)

    def out_copy(i):
        return pltpu.make_async_copy(ob.at[i], out.at[i, 0], o_sem.at[i])

    for h in (0, 2, 4, 5):
        on(h, halo_rep(h), s, lambda k, n: x_copy(h, s, k, n).wait_send())
    for h in range(1, 5):
        on(h, p, s, lambda k, n: pass_copy(h, s, k, n).wait_send())
    for h, core, both in ((0, 0, both0), (5, 1, both3)):
        @pl.when((s == core) & both)
        def _():
            for half in range(2):
                pass_copy(h, half, 0, 6).wait_send()
    for d in range(1, 8):
        pm_copy(d).wait_send()
    for m in range(4):
        sib_copy(m, s).wait_send()
    for h in range(1, 5):
        for o in range(3):
            for way in range(2):
                for a in halves(way, h):
                    ring_copy(way, h, a, o, source(way, h)).wait_send()
    final_copy.wait()
    for i in range(6):
        @pl.when(jnp.logical_not((source_of(i) == c) & (i // 2 == p)))
        def _():
            pltpu.make_async_remote_copy(
                src_ref=C.at[0], dst_ref=fin.at[i], send_sem=f_send.at[0], recv_sem=f_recv.at[i],
                device_id=right, device_id_type=MESH).wait_recv()

        keep = qm[0, i].astype(F32)
        masked = xf[i] * xm[i, w_me].astype(F32)
        ob[i] = keep * (1.5 * masked - (0.5 * norm) * fin[i].astype(F32))
        out_copy(i).start()

    for j in range(6):
        @pl.when(jnp.logical_not(targets[j][3]))
        def _():
            pltpu.make_async_remote_copy(
                src_ref=C.at[j], dst_ref=fin.at[0], send_sem=f_send.at[j], recv_sem=f_recv.at[0],
                device_id=right, device_id_type=MESH).wait_send()
    for i in range(6):
        out_copy(i).wait()


def body(x_tiles, x_mask, p_mask, q_mask):
    rows, BW, T = x_tiles.shape[0], x_tiles.shape[1], x_tiles.shape[2]
    n_rows = lax.axis_size("row")
    dma = pltpu.SemaphoreType.DMA

    def run(*refs):
        kernel(T, BW, n_rows, *refs)

    return pl.pallas_call(
        run,
        out_shape=jax.ShapeDtypeStruct((rows, 1, T, T), F32),
        in_specs=[pl.BlockSpec(memory_space=pltpu.SMEM)] * 3 + [pl.BlockSpec(memory_space=pl.ANY)],
        out_specs=pl.BlockSpec(memory_space=pl.ANY),
        scratch_shapes=[
            pltpu.VMEM((6, 6, T, T), F32),
            pltpu.VMEM((4, 6, T, T), F32),
            pltpu.VMEM((2, BW, T, T), F32),
            pltpu.VMEM((6, T, T), F32),
            pltpu.VMEM((6, 6 * T, T), BF16),
            pltpu.VMEM((4, 36 * T, T), BF16),
            pltpu.VMEM((2, T, BW * T), BF16),
            pltpu.VMEM((2, T, BW * T), BF16),
            pltpu.VMEM((8, 8, T), F32),
            pltpu.VMEM((6, T, T), BF16),
            pltpu.VMEM((6, T, T), BF16),
            pltpu.VMEM((6, T, T), F32),
            dma((6,)), dma((4,)), dma, dma, dma((6,)), dma((6, 2)), dma((4,)), dma((4,)), dma((6, 2)), dma((6, 2)),
            dma((7,)), dma((7,)),
            dma((2, 4, 6)), dma((2, 4, 6)), dma((6,)), dma((6,)), dma((6,)),
        ],
        compiler_params=pltpu.CompilerParams(
            collective_id=0, has_side_effects=True, vmem_limit_bytes=56 * 1024 * 1024),
        name="sign_step",
    )(x_mask, p_mask.T, q_mask.reshape(1, rows), x_tiles)


def solution(mesh):
    in_specs = (
        P("row", None, None, None),
        P("row", None),
        P("row", "col"),
        P("row", ("col", "rep")),
    )
    out_specs = P("row", ("col", "rep"), None, None)
    return jax.shard_map(body, mesh=mesh, in_specs=in_specs, out_specs=out_specs, check_vma=False)
```
